32 devices in a mesh: cells: 8 (over z, y), tiles: 4 (over x, core).
Axes of the slice: x: 2, y: 2, z: 4, core: 2. Of those that a mesh axis runs over, the one named last changes fastest.
Arguments:
- embeddings: bfloat16 [3, 8192, 256], P(None, 'cells'), may hold values from -6 to 6
- log_mass: float32 [3, 8192], P(None, 'cells'), may hold values from -1 to 1
- signatures: bfloat16 [8192, 256], P('cells'), may hold values from -6 to 6
- tile_list: int32 [2, 2, 1024], P(None, None, ('cells', 'tiles')), may hold values from -1 to 63, as said below
Outputs:
- early_fates: bfloat16 [8192, 256], P('cells')
- late_fates: bfloat16 [8192, 256], P('cells')
The draws below stay inside these ranges and needn't reach their ends.
Inputs may be any that keep to these rules, and one draw needn't show every extreme that they name: `tile_list`: for each coupling, slots c * 128 to c * 128 + 127 belong to owner c (an index of cells). A live slot holds a source block of owner c (blocks c * 8 to c * 8 + 7) and a target block of owner c - 1, c or c + 1; an empty slot holds -1 in both rows. Within the slots of each device the live ones come first. No pair of blocks appears twice in a coupling, every source block and every target block appears in some live slot, and one owner in each coupling has all 128 slots live.
All inputs are finite; a program needn't handle non-finite values.
Results may differ from the reference program's by a relative error of at most 0.006.
Values may be sent and summed in bfloat16 or wider, within the bound.
A program may use at most 64 MiB of HBM per device.

```python
import jax
import jax.numpy as jnp
from jax import lax

EMB = 256
FATE = 256
BLOCK = 128
SWEEPS = 2
NBLK = 8
TILE_CAP = 128
CELLS = 8192
BLOCKS = 64
N_CELLS = 8
N_TILES = 4


def owner_slots(owner_key, owner_index, live_count):
    pair_index = jnp.arange(NBLK * 3 * NBLK, dtype=jnp.int32)
    source_local = pair_index // (3 * NBLK)
    window_block = pair_index % (3 * NBLK)
    target_owner = owner_index - 1 + window_block // NBLK
    inside = (target_owner >= 0) & (target_owner < N_CELLS)
    diagonal = window_block == NBLK + source_local
    noise = jax.random.randint(owner_key, pair_index.shape, 0, 65536, dtype=jnp.int32)
    scores = noise * (3 * NBLK * NBLK) + pair_index
    scores = jnp.where(diagonal, scores + 536870912, scores)
    scores = jnp.where(inside, scores, -1 - pair_index)
    ranked = jnp.argsort(-scores)[:TILE_CAP]
    rank_index = jnp.arange(TILE_CAP, dtype=jnp.int32)
    live_mask = rank_index < live_count
    sources = jnp.where(live_mask, owner_index * NBLK + source_local[ranked], -1)
    targets = jnp.where(live_mask, (owner_index - 1) * NBLK + window_block[ranked], -1)
    share = TILE_CAP // N_TILES
    placed = rank_index % share * N_TILES + rank_index // share
    return jnp.stack([sources[placed], targets[placed]])


def draw_tile_list(key, part):
    listings = []
    for coupling in range(2):
        coupling_key = jax.random.fold_in(key, coupling + 11)
        busy_key, count_key, order_key = jax.random.split(coupling_key, 3)
        busiest = jax.random.randint(busy_key, (), 0, N_CELLS, dtype=jnp.int32)
        counts = jax.random.randint(count_key, (N_CELLS,), NBLK, 3 * TILE_CAP // 4 + 1, dtype=jnp.int32)
        owners = jnp.arange(N_CELLS, dtype=jnp.int32)
        counts = jnp.where(owners == busiest, TILE_CAP, counts)
        owner_keys = jax.random.split(order_key, N_CELLS)
        slots = jax.vmap(owner_slots)(owner_keys, owners, counts)
        listings.append(jnp.transpose(slots, (1, 0, 2)).reshape(2, N_CELLS * TILE_CAP))
    return jnp.stack(listings)


def block_scale(own_key, shape, pieces, low, largest):
    factor_of, own = 1.0, jax.random.fold_in(own_key, 6)
    for position, parts in pieces:
        steps = jnp.exp(jax.random.uniform(jax.random.fold_in(own, position), (parts,), jnp.float32, low / len(pieces), largest / len(pieces)))
        factor_of = factor_of * jnp.repeat(steps, shape[position] // parts).reshape([-1 if axis == position else 1 for axis in range(len(shape))])
    return factor_of


def scatter_about(stream_key, extent, scale, reach, pieces=(), held_as=jnp.bfloat16):
    gain = block_scale(stream_key, extent, pieces, -0.22, 0.18) if pieces else 1.0
    values = jax.random.normal(stream_key, extent, jnp.float32) * scale * gain
    return jnp.minimum(jnp.maximum(values, -reach), reach).astype(held_as)


def setup_inputs(seed: int = 0) -> dict:
    streams_of = jax.random.split(jax.random.key(seed), 5)
    return {
        "embeddings": scatter_about(streams_of[0], (3, CELLS, EMB), 1.0, 6.0, ((1, 8),)),
        "log_mass": jnp.clip(jax.random.uniform(streams_of[1], (3, CELLS), jnp.float32, -1.0, 1.0) * block_scale(streams_of[1], (3, CELLS), ((1, 8),), -0.4, 0.0), -1.0, 1.0),
        "signatures": scatter_about(streams_of[2], (CELLS, FATE), 1.0, 6.0, ((0, 8),)),
        "tile_list": draw_tile_list(jax.random.fold_in(streams_of[4], 71), 0),
    }


EPS = 0.01
RHO = 1.0
NEG = -1.0e30


def block_cost(source_rows, target_rows, source_norm, target_norm):
    crossed = jnp.dot(source_rows, target_rows.T, preferred_element_type=jnp.float32)
    return (source_norm[:, None] + target_norm[None, :] - 2.0 * crossed) / EMB


def merge_pair(first_pair, second_pair):
    highest = jnp.maximum(first_pair[0], second_pair[0])
    summed = first_pair[1] * jnp.exp(first_pair[0] - highest) + second_pair[1] * jnp.exp(second_pair[0] - highest)
    return highest, summed


def unchanged(carried, entry):
    return carried


def row_lse(sources, source_norm, targets, target_norm, target_terms, listing):
    def active_tile(carried, entry):
        highest, summed = carried
        costs = block_cost(sources[entry[0]], targets[entry[1]], source_norm[entry[0]], target_norm[entry[1]])
        scores = target_terms[entry[1]][None, :] - costs / EPS
        maxima = jnp.max(scores, axis=1)
        masses = jnp.sum(jnp.exp(scores - maxima[:, None]), axis=1)
        merged = merge_pair((highest[entry[0]], summed[entry[0]]), (maxima, masses))
        return highest.at[entry[0]].set(merged[0]), summed.at[entry[0]].set(merged[1])

    def advance(carried, entry):
        return lax.cond(entry[0] >= 0, active_tile, unchanged, carried, entry), None

    starting = (jnp.full(source_norm.shape, NEG, jnp.float32), jnp.zeros(source_norm.shape, jnp.float32))
    (highest, summed), ignored = lax.scan(advance, starting, listing.T)
    return highest + jnp.log(summed)


def col_lse(sources, source_norm, targets, target_norm, source_terms, listing):
    def active_tile(carried, entry):
        highest, summed = carried
        costs = block_cost(sources[entry[0]], targets[entry[1]], source_norm[entry[0]], target_norm[entry[1]])
        scores = source_terms[entry[0]][:, None] - costs / EPS
        maxima = jnp.max(scores, axis=0)
        masses = jnp.sum(jnp.exp(scores - maxima[None, :]), axis=0)
        merged = merge_pair((highest[entry[1]], summed[entry[1]]), (maxima, masses))
        return highest.at[entry[1]].set(merged[0]), summed.at[entry[1]].set(merged[1])

    def advance(carried, entry):
        return lax.cond(entry[0] >= 0, active_tile, unchanged, carried, entry), None

    starting = (jnp.full(target_norm.shape, NEG, jnp.float32), jnp.zeros(target_norm.shape, jnp.float32))
    (highest, summed), ignored = lax.scan(advance, starting, listing.T)
    return highest + jnp.log(summed)


def potentials(sources, targets, log_source, log_target, listing):
    source_norm = jnp.sum(sources * sources, axis=2)
    target_norm = jnp.sum(targets * targets, axis=2)
    damping = RHO / (RHO + EPS)
    potential = jnp.zeros(log_target.shape, jnp.float32)
    for sweep_index in range(SWEEPS):
        target_terms = potential / EPS + log_target
        log_total = row_lse(sources, source_norm, targets, target_norm, target_terms, listing)
        source_terms = (-damping * EPS * log_total) / EPS + log_source
        potential = -damping * EPS * col_lse(sources, source_norm, targets, target_norm, source_terms, listing)
    target_terms = potential / EPS + log_target
    log_total = row_lse(sources, source_norm, targets, target_norm, target_terms, listing)
    return target_terms, log_total


def pull(sources, targets, target_terms, log_total, listing, fate_blocks):
    source_norm = jnp.sum(sources * sources, axis=2)
    target_norm = jnp.sum(targets * targets, axis=2)

    def active_tile(carried, entry):
        costs = block_cost(sources[entry[0]], targets[entry[1]], source_norm[entry[0]], target_norm[entry[1]])
        scores = target_terms[entry[1]][None, :] - costs / EPS
        weights = jnp.exp(scores - log_total[entry[0]][:, None]).astype(jnp.bfloat16)
        product_part = jnp.dot(weights, fate_blocks[entry[1]], preferred_element_type=jnp.float32)
        return carried.at[entry[0]].add(product_part)

    def advance(carried, entry):
        return lax.cond(entry[0] >= 0, active_tile, unchanged, carried, entry), None

    starting = jnp.zeros((BLOCKS, BLOCK, fate_blocks.shape[2]), jnp.float32)
    accumulated, ignored = lax.scan(advance, starting, listing.T)
    return accumulated.reshape(-1, fate_blocks.shape[2]).astype(jnp.bfloat16)


def reference(embeddings, log_mass, signatures, tile_list):
    moments = [embeddings[moment].astype(jnp.float32).reshape(BLOCKS, BLOCK, EMB) for moment in range(3)]
    log_blocks = [log_mass[moment].reshape(BLOCKS, BLOCK) for moment in range(3)]
    states = [potentials(moments[coupling], moments[coupling + 1], log_blocks[coupling], log_blocks[coupling + 1], tile_list[coupling]) for coupling in range(2)]
    late = pull(moments[1], moments[2], states[1][0], states[1][1], tile_list[1], signatures.reshape(BLOCKS, BLOCK, FATE))
    early = pull(moments[0], moments[1], states[0][0], states[0][1], tile_list[0], late.reshape(BLOCKS, BLOCK, FATE))
    return early, late
```

```python
import functools
import math

import jax
import jax.numpy as jnp
from jax import lax
from jax.experimental import pallas as pl
from jax.experimental.pallas import tpu as pltpu
from jax.sharding import PartitionSpec as P

BLOCK = 128
SWEEPS = 2
EPS = 0.01
RHO = 1.0
NEG = -1e30
LOG2E = math.log2(math.e)
LAM = RHO / (RHO + EPS)
F32 = jnp.float32
BF16 = jnp.bfloat16
NT = (((1,), (1,)), ((), ()))


def copy_count(tiles):
    return tiles * 12 + 40


def kernel(
    tiles,
    emb,
    log_mass,
    sig,
    listing,
    early,
    late,
    xs,
    ys,
    d,
    dt,
    fates_1,
    fates_0,
    w_0,
    lists,
    lm_src,
    lm_win,
    bias,
    x_norm,
    y_norm,
    h_row,
    hb,
    ub,
    row_send,
    row_recv,
    col_send,
    col_near,
    col_far,
    part_send,
    part_recv,
    own_part,
    early_own,
    send_sem,
    recv_sem,
    local_sem,
):
    c = lax.axis_index("cells")
    t = lax.axis_index("tiles")
    n = lax.axis_size("cells")
    rows = xs.shape[1]
    depth = xs.shape[2]
    q_rows = ys.shape[2]
    n_src = rows // BLOCK
    n_q = q_rows // BLOCK
    n_tgt = 3 * n_q
    scale = LOG2E / (EPS * depth)
    t_rows = pl.ds(pl.multiple_of(t * q_rows, q_rows), q_rows)

    counter = [0]
    sends = []

    def fresh():
        counter[0] += 1
        return counter[0] - 1

    def present(offset):
        return jnp.logical_and(c + offset >= 0, c + offset < n)

    def to_tile(src, dst, step):
        i = fresh()
        copy = pltpu.make_async_remote_copy(
            src_ref=src,
            dst_ref=dst,
            send_sem=send_sem.at[i],
            recv_sem=recv_sem.at[i],
            device_id={"tiles": lax.rem(t + step, tiles)},
            device_id_type=pl.DeviceIdType.MESH,
        )
        copy.start()
        sends.append((copy, None))
        return copy.wait_recv

    def to_cell(src, dst, offset):
        i = fresh()
        copy = pltpu.make_async_remote_copy(
            src_ref=src,
            dst_ref=dst,
            send_sem=send_sem.at[i],
            recv_sem=recv_sem.at[i],
            device_id={"cells": c + offset},
            device_id_type=pl.DeviceIdType.MESH,
        )

        @pl.when(present(offset))
        def _():
            copy.start()

        sends.append((copy, offset))

        def wait():
            @pl.when(present(-offset))
            def _():
                copy.wait_recv()

        return wait

    for offset, part in ((1, 0), (-1, 2)):

        @pl.when(jnp.logical_not(present(-offset)))
        def _(part=part):
            for k in range(2):
                ys[k, part] = jnp.zeros(ys.shape[2:], BF16)
            fates_1[part] = jnp.zeros(fates_1.shape[1:], BF16)
            fates_0[part] = jnp.zeros(fates_0.shape[1:], BF16)
            lm_win[part] = jnp.zeros(lm_win.shape[1:], F32)

    for buffer in (col_near, col_far):
        buffer[:, :, :, :, 0] = jnp.full(buffer.shape[:4] + buffer.shape[5:], NEG, F32)
        buffer[:, :, :, :, 1] = jnp.zeros(buffer.shape[:4] + buffer.shape[5:], F32)
    col_send[:, :, :, 0] = jnp.full(col_send.shape[:3] + col_send.shape[4:], NEG, F32)
    col_send[:, :, :, 1] = jnp.ones(col_send.shape[:3] + col_send.shape[4:], F32)

    barrier = pltpu.get_barrier_semaphore()
    for step in range(1, tiles):
        pl.semaphore_signal(
            barrier, inc=1, device_id={"tiles": lax.rem(t + step, tiles)}, device_id_type=pl.DeviceIdType.MESH
        )
    for offset in (1, -1, 2, -2):

        @pl.when(present(offset))
        def _(offset=offset):
            pl.semaphore_signal(
                barrier, inc=1, device_id={"cells": c + offset}, device_id_type=pl.DeviceIdType.MESH
            )

    local = []
    for i, (src, dst) in enumerate(
        (
            (emb.at[1], xs.at[1]),
            (emb.at[2, t_rows], ys.at[1, 1]),
            (emb.at[0], xs.at[0]),
            (emb.at[1, t_rows], ys.at[0, 1]),
            (sig.at[t_rows], fates_1.at[1]),
        )
    ):
        copy = pltpu.make_async_copy(src, dst, local_sem.at[i])
        copy.start()
        local.append(copy)

    lm_src[...] = jnp.zeros(lm_src.shape, F32)
    for k in range(2):
        for q in range(n_q):
            lanes = pl.ds(pl.multiple_of((t * n_q + q) * BLOCK, BLOCK), BLOCK)
            lm_src[k, q : q + 1, :] = log_mass[k + 1 : k + 2, lanes] * LOG2E
    lm_win[1] = lm_src[...]

    peers = sum(present(offset).astype(jnp.int32) for offset in (1, -1, 2, -2))
    pl.semaphore_wait(barrier, tiles - 1 + peers)

    list_waits = [to_tile(listing, lists.at[step], step) for step in range(1, tiles)]
    near = ((1, 0), (-1, 2))
    lm_waits = [to_cell(lm_src, lm_win.at[part], offset) for offset, part in near]
    y_waits = [None, None]
    y_waits[1] = [to_cell(emb.at[2, t_rows], ys.at[1, part], offset) for offset, part in near]
    y_waits[0] = [to_cell(emb.at[1, t_rows], ys.at[0, part], offset) for offset, part in near]
    sig_waits = [to_cell(sig.at[t_rows], fates_1.at[part], offset) for offset, part in near]

    lists[0] = listing[...]
    for wait in list_waits:
        wait()

    pair = lax.broadcasted_iota(jnp.int32, (n_src * n_tgt, 1), 0)
    src_id = c * n_src + pair // n_tgt
    slot = pair % n_tgt
    tgt_id = (c - 1 + slot // n_q) * n_src + t * n_q + slot % n_q
    for k in range(2):
        found = jnp.zeros((n_src * n_tgt, 1), F32)
        for step in range(tiles):
            hit = jnp.logical_and(
                lists[step, k, 0:1, :] == src_id, lists[step, k, 1:2, :] == tgt_id
            )
            found = found + jnp.sum(jnp.where(hit, 1.0, 0.0), axis=1, keepdims=True)
        bias[k] = jnp.broadcast_to(jnp.where(found > 0.0, 0.0, NEG), (n_src * n_tgt, BLOCK))

    ones = jnp.ones((8, depth), BF16)

    def norm_rows(block):
        wide = block.astype(F32)
        square = wide * wide
        high = square.astype(BF16)
        low = (square - high.astype(F32)).astype(BF16)
        return scale * (
            lax.dot_general(ones, high, NT, preferred_element_type=F32)
            + lax.dot_general(ones, low, NT, preferred_element_type=F32)
        )

    def source_norms(k):
        @pl.loop(0, n_src)
        def _(b):
            x_norm[k, pl.ds(b, 1), :] = norm_rows(xs[k, pl.ds(pl.multiple_of(b * BLOCK, BLOCK), BLOCK), :])[0:1]

    def products(k, part):
        y = ys[k, part]
        norms = norm_rows(y)
        for q in range(n_q):
            y_norm[k, part, q : q + 1, :] = norms[0:1, q * BLOCK : (q + 1) * BLOCK]

        @pl.loop(0, n_src)
        def _(b):
            block = pl.ds(pl.multiple_of(b * BLOCK, BLOCK), BLOCK)
            x = xs[k, block, :]
            cross = lax.dot_general(x, y, NT, preferred_element_type=F32) * (2.0 * scale)
            crossed = lax.dot_general(y, x, NT, preferred_element_type=F32) * (2.0 * scale)
            for q in range(n_q):
                j = part * n_q + q
                shift = bias[k, pl.ds(b * n_tgt + j, 1), :]
                d[k, j, block, :] = cross[:, q * BLOCK : (q + 1) * BLOCK] + shift
                dt[k, b, j * BLOCK : (j + 1) * BLOCK, :] = crossed[q * BLOCK : (q + 1) * BLOCK] + shift

    def down(row):
        return jnp.transpose(jnp.broadcast_to(row, (BLOCK, BLOCK)))

    def row_pass(k, phase):
        for j in range(n_tgt):
            hb[k, j * BLOCK : (j + 1) * BLOCK, :] = down(h_row[k, j // n_q, j % n_q : j % n_q + 1, :])

        @pl.loop(0, n_src)
        def _(b):
            scores = hb[k] + dt[k, b]
            highest = jnp.max(scores, axis=0, keepdims=True)
            row_send[k, phase, 0, pl.ds(b, 1), :] = highest
            row_send[k, phase, 1, pl.ds(b, 1), :] = jnp.sum(jnp.exp2(scores - highest), axis=0, keepdims=True)

        return [
            to_tile(row_send.at[k, phase], row_recv.at[k, phase, step - 1], step) for step in range(1, tiles)
        ]

    def merged(pairs):
        highest = functools.reduce(jnp.maximum, [pair[0] for pair in pairs])
        total = sum(pair[1] * jnp.exp2(pair[0] - highest) for pair in pairs)
        return highest + jnp.log(total) * LOG2E

    def row_total(k, phase, waits):
        for wait in waits:
            wait()
        pairs = [(row_send[k, phase, 0], row_send[k, phase, 1])]
        pairs += [(row_recv[k, phase, s, 0], row_recv[k, phase, s, 1]) for s in range(tiles - 1)]
        return merged(pairs)

    def spread(k, values):
        for b in range(n_src):
            ub[k, b * BLOCK : (b + 1) * BLOCK, :] = down(values[b : b + 1])

    def col_pass(k, phase, total):
        mass = jnp.concatenate(
            [log_mass[k : k + 1, b * BLOCK : (b + 1) * BLOCK] for b in range(n_src)], axis=0
        )
        spread(k, mass * LOG2E - LAM * total + (LAM - 1.0) * x_norm[k])

        @pl.loop(0, 3)
        def _(part):
            for q in range(n_q):
                scores = ub[k] + d[k, part * n_q + q]
                highest = jnp.max(scores, axis=0, keepdims=True)
                col_send[k, phase, part, 0, q : q + 1, :] = highest
                col_send[k, phase, part, 1, q : q + 1, :] = jnp.sum(
                    jnp.exp2(scores - highest), axis=0, keepdims=True
                )

        mine = col_send.at[k, phase]
        return [
            to_cell(mine.at[pl.ds(1, 2)], col_near.at[k, phase, 0], 1),
            to_cell(mine.at[pl.ds(0, 2)], col_near.at[k, phase, 1], -1),
            to_cell(mine.at[pl.ds(2, 1)], col_far.at[k, phase, 0], 2),
            to_cell(mine.at[pl.ds(0, 1)], col_far.at[k, phase, 1], -2),
        ]

    def col_total(k, phase, waits):
        for wait in waits:
            wait()

        def pair(ref):
            return ref[0], ref[1]

        mine = col_send.at[k, phase]
        below, above = col_near.at[k, phase, 0], col_near.at[k, phase, 1]
        far_below, far_above = col_far.at[k, phase, 0, 0], col_far.at[k, phase, 1, 0]
        totals = (
            merged([pair(far_below), pair(below.at[0]), pair(mine.at[0])]),
            merged([pair(below.at[1]), pair(mine.at[1]), pair(above.at[0])]),
            merged([pair(mine.at[2]), pair(above.at[1]), pair(far_above)]),
        )
        for part in range(3):
            h_row[k, part] = lm_win[part, k] - LAM * totals[part] + (LAM - 1.0) * y_norm[k, part]

    y_norm[...] = jnp.zeros(y_norm.shape, F32)
    local[0].wait()
    local[1].wait()
    source_norms(1)
    products(1, 1)
    local[2].wait()
    local[3].wait()
    source_norms(0)
    products(0, 1)
    for wait in lm_waits:
        wait()
    row_waits, col_waits = {}, {}
    for k in (1, 0):
        for wait, (_, part) in zip(y_waits[k], near):
            wait()
            products(k, part)
        for part in range(3):
            h_row[k, part] = lm_win[part, k] - y_norm[k, part]
        row_waits[k] = row_pass(k, 0)
    for sweep in range(SWEEPS):
        for k in (1, 0):
            col_waits[k] = col_pass(k, sweep, row_total(k, sweep, row_waits[k]))
        for k in (1, 0):
            col_total(k, sweep, col_waits[k])
            row_waits[k] = row_pass(k, sweep + 1)

    def weights(k, block, part):
        return jnp.concatenate(
            [
                jnp.exp2(
                    h_row[k, part, q : q + 1, :] + d[k, part * n_q + q, block, :] - ub[k, block, :]
                ).astype(BF16)
                for q in range(n_q)
            ],
            axis=1,
        )

    def row_block(index):
        return pl.ds(pl.multiple_of(index * q_rows, q_rows), q_rows)

    spread(1, row_total(1, SWEEPS, row_waits[1]))
    local[4].wait()
    for wait in sig_waits:
        wait()
    part_waits = []
    for step in range(1, tiles + 1):
        block = row_block(lax.rem(t + step, tiles))
        total = sum(
            jnp.dot(weights(1, block, part), fates_1[part], preferred_element_type=F32) for part in range(3)
        )
        if step < tiles:
            part_send[1, step - 1] = total.astype(BF16)
            part_waits.append(to_tile(part_send.at[1, step - 1], part_recv.at[1, step - 1], step))
        else:
            own_part[...] = total

    spread(0, row_total(0, SWEEPS, row_waits[0]))

    @pl.loop(0, tiles)
    def _(r):
        block = row_block(r)
        for part in range(3):
            w_0[part, block, :] = weights(0, block, part)

    for wait in part_waits:
        wait()
    fates_0[1] = (
        own_part[...] + sum(part_recv[1, s].astype(F32) for s in range(tiles - 1))
    ).astype(BF16)
    late_waits = [to_cell(fates_0.at[1], fates_0.at[part], offset) for offset, part in near]
    gather_waits = [to_tile(fates_0.at[1], late.at[t_rows], step) for step in range(1, tiles)]
    late[t_rows, :] = fates_0[1]

    for wait in late_waits:
        wait()
    part_waits = []
    for step in range(1, tiles + 1):
        block = row_block(lax.rem(t + step, tiles))
        total = sum(
            jnp.dot(w_0[part, block, :], fates_0[part], preferred_element_type=F32) for part in range(3)
        )
        if step < tiles:
            part_send[0, step - 1] = total.astype(BF16)
            part_waits.append(to_tile(part_send.at[0, step - 1], part_recv.at[0, step - 1], step))
        else:
            own_part[...] = total
    for wait in part_waits:
        wait()
    early_own[...] = (
        own_part[...] + sum(part_recv[0, s].astype(F32) for s in range(tiles - 1))
    ).astype(BF16)
    gather_waits += [to_tile(early_own, early.at[t_rows], step) for step in range(1, tiles)]
    early[t_rows, :] = early_own[...]
    for wait in gather_waits:
        wait()
    for copy, offset in sends:
        if offset is None:
            copy.wait_send()
        else:

            @pl.when(present(offset))
            def _(copy=copy):
                copy.wait_send()


def on_device(tiles, embeddings, log_mass, signatures, tile_list):
    _, rows, depth = embeddings.shape
    fate = signatures.shape[1]
    q_rows = rows // tiles
    n_src = rows // BLOCK
    n_q = q_rows // BLOCK
    n_tgt = 3 * n_q
    vmem = pltpu.VMEM
    copies = copy_count(tiles)
    return pl.pallas_call(
        functools.partial(kernel, tiles),
        out_shape=(
            jax.ShapeDtypeStruct((rows, fate), BF16),
            jax.ShapeDtypeStruct((rows, fate), BF16),
        ),
        in_specs=[
            pl.BlockSpec(memory_space=pl.ANY),
            pl.BlockSpec(memory_space=vmem),
            pl.BlockSpec(memory_space=pl.ANY),
            pl.BlockSpec(memory_space=vmem),
        ],
        out_specs=(pl.BlockSpec(memory_space=vmem), pl.BlockSpec(memory_space=vmem)),
        scratch_shapes=[
            vmem((2, rows, depth), BF16),
            vmem((2, 3, q_rows, depth), BF16),
            vmem((2, n_tgt, rows, BLOCK), F32),
            vmem((2, n_src, n_tgt * BLOCK, BLOCK), F32),
            vmem((3, q_rows, fate), BF16),
            vmem((3, q_rows, fate), BF16),
            vmem((3, rows, q_rows), BF16),
            vmem((tiles,) + tile_list.shape, jnp.int32),
            vmem((2, 8, BLOCK), F32),
            vmem((3, 2, 8, BLOCK), F32),
            vmem((2, n_src * n_tgt, BLOCK), F32),
            vmem((2, n_src, BLOCK), F32),
            vmem((2, 3, 8, BLOCK), F32),
            vmem((2, 3, 8, BLOCK), F32),
            vmem((2, n_tgt * BLOCK, BLOCK), F32),
            vmem((2, rows, BLOCK), F32),
            vmem((2, SWEEPS + 1, 2, n_src, BLOCK), F32),
            vmem((2, SWEEPS + 1, tiles - 1, 2, n_src, BLOCK), F32),
            vmem((2, SWEEPS, 3, 2, 8, BLOCK), F32),
            vmem((2, SWEEPS, 2, 2, 2, 8, BLOCK), F32),
            vmem((2, SWEEPS, 2, 1, 2, 8, BLOCK), F32),
            vmem((2, tiles - 1, q_rows, fate), BF16),
            vmem((2, tiles - 1, q_rows, fate), BF16),
            vmem((q_rows, fate), F32),
            vmem((q_rows, fate), BF16),
            pltpu.SemaphoreType.DMA((copies,)),
            pltpu.SemaphoreType.DMA((copies,)),
            pltpu.SemaphoreType.DMA((5,)),
        ],
        compiler_params=pltpu.CompilerParams(
            collective_id=0, has_side_effects=True, vmem_limit_bytes=44 * 1024 * 1024
        ),
    )(embeddings, log_mass, signatures, tile_list)


def solution(mesh):
    in_specs = (
        P(None, "cells", None),
        P(None, "cells"),
        P("cells", None),
        P(None, None, ("cells", "tiles")),
    )
    out_specs = (P("cells", None), P("cells", None))
    return jax.shard_map(
        functools.partial(on_device, mesh.shape["tiles"]),
        mesh=mesh,
        in_specs=in_specs,
        out_specs=out_specs,
        check_vma=False,
    )
```

```python
import functools
import math

import jax
import jax.numpy as jnp
from jax import lax
from jax.experimental import pallas as pl
from jax.experimental.pallas import tpu as pltpu
from jax.sharding import PartitionSpec as P

BLOCK = 128
SWEEPS = 2
EPS = 0.01
RHO = 1.0
NEG = -1e30
LOG2E = math.log2(math.e)
LAM = RHO / (RHO + EPS)
F32 = jnp.float32
BF16 = jnp.bfloat16
NT = (((1,), (1,)), ((), ()))


def copy_count(tiles):
    return tiles * 12 + 40


def kernel(
    tiles,
    emb,
    log_mass,
    sig,
    listing,
    early,
    late,
    xs,
    ys,
    d,
    dt,
    fates_1,
    fates_0,
    w_0,
    lists,
    lm_src,
    lm_win,
    bias,
    x_norm,
    y_norm,
    h_row,
    hb,
    ub,
    row_send,
    row_recv,
    col_send,
    col_near,
    col_far,
    a_send,
    a_recv,
    b_send,
    b_recv,
    kept,
    early_own,
    send_sem,
    recv_sem,
    local_sem,
):
    c = lax.axis_index("cells")
    t = lax.axis_index("tiles")
    n = lax.axis_size("cells")
    rows = xs.shape[1]
    depth = xs.shape[2]
    q_rows = ys.shape[2]
    n_src = rows // BLOCK
    n_q = q_rows // BLOCK
    n_tgt = 3 * n_q
    scale = LOG2E / (EPS * depth)
    t_rows = pl.ds(pl.multiple_of(t * q_rows, q_rows), q_rows)

    counter = [0]
    sends = []

    def fresh():
        counter[0] += 1
        return counter[0] - 1

    def present(offset):
        return jnp.logical_and(c + offset >= 0, c + offset < n)

    def to_tile(src, dst, step):
        return to_peer(src, dst, lax.rem(t + step, tiles))

    def to_peer(src, dst, peer):
        i = fresh()
        copy = pltpu.make_async_remote_copy(
            src_ref=src,
            dst_ref=dst,
            send_sem=send_sem.at[i],
            recv_sem=recv_sem.at[i],
            device_id={"tiles": peer},
            device_id_type=pl.DeviceIdType.MESH,
        )
        copy.start()
        sends.append((copy, None))
        return copy.wait_recv

    def to_cell(src, dst, offset):
        i = fresh()
        copy = pltpu.make_async_remote_copy(
            src_ref=src,
            dst_ref=dst,
            send_sem=send_sem.at[i],
            recv_sem=recv_sem.at[i],
            device_id={"cells": c + offset},
            device_id_type=pl.DeviceIdType.MESH,
        )

        @pl.when(present(offset))
        def _():
            copy.start()

        sends.append((copy, offset))

        def wait():
            @pl.when(present(-offset))
            def _():
                copy.wait_recv()

        return wait

    for offset, part in ((1, 0), (-1, 2)):

        @pl.when(jnp.logical_not(present(-offset)))
        def _(part=part):
            for k in range(2):
                ys[k, part] = jnp.zeros(ys.shape[2:], BF16)
            fates_1[part] = jnp.zeros(fates_1.shape[1:], BF16)
            for f in range(2):
                fates_0[f, part] = jnp.zeros(fates_0.shape[2:], BF16)
            lm_win[part] = jnp.zeros(lm_win.shape[1:], F32)

    for buffer in (col_near, col_far):
        buffer[:, :, :, :, 0] = jnp.full(buffer.shape[:4] + buffer.shape[5:], NEG, F32)
        buffer[:, :, :, :, 1] = jnp.zeros(buffer.shape[:4] + buffer.shape[5:], F32)
    col_send[:, :, :, 0] = jnp.full(col_send.shape[:3] + col_send.shape[4:], NEG, F32)
    col_send[:, :, :, 1] = jnp.ones(col_send.shape[:3] + col_send.shape[4:], F32)

    barrier = pltpu.get_barrier_semaphore()
    for step in range(1, tiles):
        pl.semaphore_signal(
            barrier, inc=1, device_id={"tiles": lax.rem(t + step, tiles)}, device_id_type=pl.DeviceIdType.MESH
        )
    for offset in (1, -1, 2, -2):

        @pl.when(present(offset))
        def _(offset=offset):
            pl.semaphore_signal(
                barrier, inc=1, device_id={"cells": c + offset}, device_id_type=pl.DeviceIdType.MESH
            )

    local = []
    for i, (src, dst) in enumerate(
        (
            (emb.at[1], xs.at[1]),
            (emb.at[2, t_rows], ys.at[1, 1]),
            (emb.at[0], xs.at[0]),
            (emb.at[1, t_rows], ys.at[0, 1]),
            (sig.at[t_rows], fates_1.at[1]),
        )
    ):
        copy = pltpu.make_async_copy(src, dst, local_sem.at[i])
        copy.start()
        local.append(copy)

    lm_src[...] = jnp.zeros(lm_src.shape, F32)
    for k in range(2):
        for q in range(n_q):
            lanes = pl.ds(pl.multiple_of((t * n_q + q) * BLOCK, BLOCK), BLOCK)
            lm_src[k, q : q + 1, :] = log_mass[k + 1 : k + 2, lanes] * LOG2E
    lm_win[1] = lm_src[...]

    peers = sum(present(offset).astype(jnp.int32) for offset in (1, -1, 2, -2))
    pl.semaphore_wait(barrier, tiles - 1 + peers)

    list_waits = [to_tile(listing, lists.at[step], step) for step in range(1, tiles)]
    near = ((1, 0), (-1, 2))
    lm_waits = [to_cell(lm_src, lm_win.at[part], offset) for offset, part in near]
    y_waits = [None, None]
    y_waits[1] = [to_cell(emb.at[2, t_rows], ys.at[1, part], offset) for offset, part in near]

    lists[0] = listing[...]
    for wait in list_waits:
        wait()

    pair = lax.broadcasted_iota(jnp.int32, (n_src * n_tgt, 1), 0)
    src_id = c * n_src + pair // n_tgt
    slot = pair % n_tgt
    tgt_id = (c - 1 + slot // n_q) * n_src + t * n_q + slot % n_q
    for k in range(2):
        found = jnp.zeros((n_src * n_tgt, 1), F32)
        for step in range(tiles):
            hit = jnp.logical_and(
                lists[step, k, 0:1, :] == src_id, lists[step, k, 1:2, :] == tgt_id
            )
            found = found + jnp.sum(jnp.where(hit, 1.0, 0.0), axis=1, keepdims=True)
        bias[k] = jnp.broadcast_to(jnp.where(found > 0.0, 0.0, NEG), (n_src * n_tgt, BLOCK))

    ones = jnp.ones((8, depth), BF16)

    def norm_rows(block):
        wide = block.astype(F32)
        square = wide * wide
        high = square.astype(BF16)
        low = (square - high.astype(F32)).astype(BF16)
        return scale * (
            lax.dot_general(ones, high, NT, preferred_element_type=F32)
            + lax.dot_general(ones, low, NT, preferred_element_type=F32)
        )

    def source_norms(k):
        @pl.loop(0, n_src)
        def _(b):
            x_norm[k, pl.ds(b, 1), :] = norm_rows(xs[k, pl.ds(pl.multiple_of(b * BLOCK, BLOCK), BLOCK), :])[0:1]

    def products(k, part):
        y = ys[k, part]
        norms = norm_rows(y)
        for q in range(n_q):
            y_norm[k, part, q : q + 1, :] = norms[0:1, q * BLOCK : (q + 1) * BLOCK]

        @pl.loop(0, n_src)
        def _(b):
            block = pl.ds(pl.multiple_of(b * BLOCK, BLOCK), BLOCK)
            x = xs[k, block, :]
            cross = lax.dot_general(x, y, NT, preferred_element_type=F32) * (2.0 * scale)
            crossed = lax.dot_general(y, x, NT, preferred_element_type=F32) * (2.0 * scale)
            for q in range(n_q):
                j = part * n_q + q
                shift = bias[k, pl.ds(b * n_tgt + j, 1), :]
                d[k, j, block, :] = cross[:, q * BLOCK : (q + 1) * BLOCK] + shift
                dt[k, b, j * BLOCK : (j + 1) * BLOCK, :] = crossed[q * BLOCK : (q + 1) * BLOCK] + shift

    def down(row):
        return jnp.transpose(jnp.broadcast_to(row, (BLOCK, BLOCK)))

    def row_pass(k, phase):
        for j in range(n_tgt):
            hb[k, j * BLOCK : (j + 1) * BLOCK, :] = down(h_row[k, j // n_q, j % n_q : j % n_q + 1, :])

        @pl.loop(0, n_src)
        def _(b):
            scores = hb[k] + dt[k, b]
            highest = jnp.max(scores, axis=0, keepdims=True)
            row_send[k, phase, 0, pl.ds(b, 1), :] = highest
            row_send[k, phase, 1, pl.ds(b, 1), :] = jnp.sum(jnp.exp2(scores - highest), axis=0, keepdims=True)

        return [
            to_tile(row_send.at[k, phase], row_recv.at[k, phase, step - 1], step) for step in range(1, tiles)
        ]

    def merged(pairs):
        highest = functools.reduce(jnp.maximum, [pair[0] for pair in pairs])
        total = sum(pair[1] * jnp.exp2(pair[0] - highest) for pair in pairs)
        return highest + jnp.log(total) * LOG2E

    def row_total(k, phase, waits):
        for wait in waits:
            wait()
        pairs = [(row_send[k, phase, 0], row_send[k, phase, 1])]
        pairs += [(row_recv[k, phase, s, 0], row_recv[k, phase, s, 1]) for s in range(tiles - 1)]
        return merged(pairs)

    def spread(k, values):
        for b in range(n_src):
            ub[k, b * BLOCK : (b + 1) * BLOCK, :] = down(values[b : b + 1])

    def col_pass(k, phase, total):
        mass = jnp.concatenate(
            [log_mass[k : k + 1, b * BLOCK : (b + 1) * BLOCK] for b in range(n_src)], axis=0
        )
        spread(k, mass * LOG2E - LAM * total + (LAM - 1.0) * x_norm[k])

        @pl.loop(0, 3)
        def _(part):
            for q in range(n_q):
                scores = ub[k] + d[k, part * n_q + q]
                highest = jnp.max(scores, axis=0, keepdims=True)
                col_send[k, phase, part, 0, q : q + 1, :] = highest
                col_send[k, phase, part, 1, q : q + 1, :] = jnp.sum(
                    jnp.exp2(scores - highest), axis=0, keepdims=True
                )

        mine = col_send.at[k, phase]
        return [
            to_cell(mine.at[pl.ds(1, 2)], col_near.at[k, phase, 0], 1),
            to_cell(mine.at[pl.ds(0, 2)], col_near.at[k, phase, 1], -1),
            to_cell(mine.at[pl.ds(2, 1)], col_far.at[k, phase, 0], 2),
            to_cell(mine.at[pl.ds(0, 1)], col_far.at[k, phase, 1], -2),
        ]

    def col_total(k, phase, waits):
        for wait in waits:
            wait()

        def pair(ref):
            return ref[0], ref[1]

        mine = col_send.at[k, phase]
        below, above = col_near.at[k, phase, 0], col_near.at[k, phase, 1]
        far_below, far_above = col_far.at[k, phase, 0, 0], col_far.at[k, phase, 1, 0]
        totals = (
            merged([pair(far_below), pair(below.at[0]), pair(mine.at[0])]),
            merged([pair(below.at[1]), pair(mine.at[1]), pair(above.at[0])]),
            merged([pair(mine.at[2]), pair(above.at[1]), pair(far_above)]),
        )
        for part in range(3):
            h_row[k, part] = lm_win[part, k] - LAM * totals[part] + (LAM - 1.0) * y_norm[k, part]

    y_norm[...] = jnp.zeros(y_norm.shape, F32)
    local[0].wait()
    local[1].wait()
    source_norms(1)
    products(1, 1)
    local[2].wait()
    local[3].wait()
    source_norms(0)
    products(0, 1)
    for wait in lm_waits:
        wait()
    row_waits, col_waits = {}, {}
    for k in (1, 0):
        for wait in y_waits[k]:
            wait()
        if k == 1:
            y_waits[0] = [to_cell(emb.at[1, t_rows], ys.at[0, part], offset) for offset, part in near]
        else:
            sig_waits = [to_cell(sig.at[t_rows], fates_1.at[part], offset) for offset, part in near]
        for _, part in near:
            products(k, part)
        for part in range(3):
            h_row[k, part] = lm_win[part, k] - y_norm[k, part]
        row_waits[k] = row_pass(k, 0)
    for sweep in range(SWEEPS):
        for k in (1, 0):
            col_waits[k] = col_pass(k, sweep, row_total(k, sweep, row_waits[k]))
        for k in (1, 0):
            col_total(k, sweep, col_waits[k])
            row_waits[k] = row_pass(k, sweep + 1)

    def weights(k, block, part):
        return jnp.concatenate(
            [
                jnp.exp2(
                    h_row[k, part, q : q + 1, :] + d[k, part * n_q + q, block, :] - ub[k, block, :]
                ).astype(BF16)
                for q in range(n_q)
            ],
            axis=1,
        )

    def row_block(index):
        return pl.ds(pl.multiple_of(index * q_rows, q_rows), q_rows)

    spread(1, row_total(1, SWEEPS, row_waits[1]))
    local[4].wait()
    for wait in sig_waits:
        wait()
    t_1 = t + 1 - 2 * lax.rem(t, 2)
    t_2 = lax.rem(t + 2, tiles)
    t_3 = lax.rem(t_1 + 2, tiles)
    half = fates_0.shape[3]
    lanes = [slice(f * half, (f + 1) * half) for f in range(2)]

    def late_part(index):
        block = row_block(index)
        return sum(
            jnp.dot(weights(1, block, part), fates_1[part], preferred_element_type=F32) for part in range(3)
        )

    def early_part(index, f):
        block = row_block(index)
        return sum(
            jnp.dot(w_0[part, block, :], fates_0[f, part], preferred_element_type=F32) for part in range(3)
        )

    def to_mate(k, f):
        return to_peer(a_send.at[k, f], a_recv.at[k, f], t_1)

    def across(k, f, arrived):
        arrived()
        b_send[k, f] = (kept[k, f, 1] + a_recv[k, f, 1].astype(F32)).astype(BF16)
        return to_peer(b_send.at[k, f], b_recv.at[k, f], t_2)

    def summed(k, f, arrived):
        arrived()
        return (kept[k, f, 0] + a_recv[k, f, 0].astype(F32) + b_recv[k, f].astype(F32)).astype(BF16)

    def gather(block, out, f):
        here = out.at[t_rows, lanes[f]]
        return to_peer(block, here, t_1), to_peer(block, here, t_2)

    def forward(waits, out, f):
        waits[1]()
        there = out.at[row_block(t_2), lanes[f]]
        return [waits[0], to_peer(there, there, t_1)]

    for i, index in enumerate((t_1, t_3)):
        total = late_part(index)
        for f in range(2):
            a_send[1, f, i] = total[:, lanes[f]].astype(BF16)
    a_waits = [to_mate(1, f) for f in range(2)]
    for i, index in enumerate((t, t_2)):
        total = late_part(index)
        for f in range(2):
            kept[1, f, i] = total[:, lanes[f]]
    b_waits = [across(1, f, a_waits[f]) for f in range(2)]

    spread(0, row_total(0, SWEEPS, row_waits[0]))

    @pl.loop(0, tiles)
    def _(r):
        block = row_block(r)
        for part in range(3):
            w_0[part, block, :] = weights(0, block, part)

    late_waits, late_gather = [], []
    for f in range(2):
        fates_0[f, 1] = summed(1, f, b_waits[f])
        late_waits.append([to_cell(fates_0.at[f, 1], fates_0.at[f, part], offset) for offset, part in near])
        late_gather.append(gather(fates_0.at[f, 1], late, f))
        late[t_rows, lanes[f]] = fates_0[f, 1]

    b_waits = []
    for f in range(2):
        for wait in late_waits[f]:
            wait()
        for i, index in enumerate((t_1, t_3)):
            a_send[0, f, i] = early_part(index, f).astype(BF16)
        arrived = to_mate(0, f)
        for i, index in enumerate((t, t_2)):
            kept[0, f, i] = early_part(index, f)
        b_waits.append(across(0, f, arrived))
    gather_waits = []
    for f in range(2):
        gather_waits += forward(late_gather[f], late, f)
    early_gather = []
    for f in range(2):
        early_own[f] = summed(0, f, b_waits[f])
        early_gather.append(gather(early_own.at[f], early, f))
        early[t_rows, lanes[f]] = early_own[f]
    for f in range(2):
        gather_waits += forward(early_gather[f], early, f)
    for wait in gather_waits:
        wait()
    for copy, offset in sends:
        if offset is None:
            copy.wait_send()
        else:

            @pl.when(present(offset))
            def _(copy=copy):
                copy.wait_send()


def on_device(tiles, embeddings, log_mass, signatures, tile_list):
    _, rows, depth = embeddings.shape
    fate = signatures.shape[1]
    q_rows = rows // tiles
    n_src = rows // BLOCK
    n_q = q_rows // BLOCK
    n_tgt = 3 * n_q
    vmem = pltpu.VMEM
    copies = copy_count(tiles)
    return pl.pallas_call(
        functools.partial(kernel, tiles),
        out_shape=(
            jax.ShapeDtypeStruct((rows, fate), BF16),
            jax.ShapeDtypeStruct((rows, fate), BF16),
        ),
        in_specs=[
            pl.BlockSpec(memory_space=pl.ANY),
            pl.BlockSpec(memory_space=vmem),
            pl.BlockSpec(memory_space=pl.ANY),
            pl.BlockSpec(memory_space=vmem),
        ],
        out_specs=(pl.BlockSpec(memory_space=vmem), pl.BlockSpec(memory_space=vmem)),
        scratch_shapes=[
            vmem((2, rows, depth), BF16),
            vmem((2, 3, q_rows, depth), BF16),
            vmem((2, n_tgt, rows, BLOCK), F32),
            vmem((2, n_src, n_tgt * BLOCK, BLOCK), F32),
            vmem((3, q_rows, fate), BF16),
            vmem((2, 3, q_rows, fate // 2), BF16),
            vmem((3, rows, q_rows), BF16),
            vmem((tiles,) + tile_list.shape, jnp.int32),
            vmem((2, 8, BLOCK), F32),
            vmem((3, 2, 8, BLOCK), F32),
            vmem((2, n_src * n_tgt, BLOCK), F32),
            vmem((2, n_src, BLOCK), F32),
            vmem((2, 3, 8, BLOCK), F32),
            vmem((2, 3, 8, BLOCK), F32),
            vmem((2, n_tgt * BLOCK, BLOCK), F32),
            vmem((2, rows, BLOCK), F32),
            vmem((2, SWEEPS + 1, 2, n_src, BLOCK), F32),
            vmem((2, SWEEPS + 1, tiles - 1, 2, n_src, BLOCK), F32),
            vmem((2, SWEEPS, 3, 2, 8, BLOCK), F32),
            vmem((2, SWEEPS, 2, 2, 2, 8, BLOCK), F32),
            vmem((2, SWEEPS, 2, 1, 2, 8, BLOCK), F32),
            vmem((2, 2, 2, q_rows, fate // 2), BF16),
            vmem((2, 2, 2, q_rows, fate // 2), BF16),
            vmem((2, 2, q_rows, fate // 2), BF16),
            vmem((2, 2, q_rows, fate // 2), BF16),
            vmem((2, 2, 2, q_rows, fate // 2), F32),
            vmem((2, q_rows, fate // 2), BF16),
            pltpu.SemaphoreType.DMA((copies,)),
            pltpu.SemaphoreType.DMA((copies,)),
            pltpu.SemaphoreType.DMA((5,)),
        ],
        compiler_params=pltpu.CompilerParams(
            collective_id=0, has_side_effects=True, vmem_limit_bytes=44 * 1024 * 1024
        ),
    )(embeddings, log_mass, signatures, tile_list)


def solution(mesh):
    in_specs = (
        P(None, "cells", None),
        P(None, "cells"),
        P("cells", None),
        P(None, None, ("cells", "tiles")),
    )
    out_specs = (P("cells", None), P("cells", None))
    return jax.shard_map(
        functools.partial(on_device, mesh.shape["tiles"]),
        mesh=mesh,
        in_specs=in_specs,
        out_specs=out_specs,
        check_vma=False,
    )
```

```python
import functools
import math

import jax
import jax.numpy as jnp
from jax import lax
from jax.experimental import pallas as pl
from jax.experimental.pallas import tpu as pltpu
from jax.sharding import PartitionSpec as P

BLOCK = 128
SWEEPS = 2
EPS = 0.01
RHO = 1.0
NEG = -1e30
LOG2E = math.log2(math.e)
LAM = RHO / (RHO + EPS)
F32 = jnp.float32
BF16 = jnp.bfloat16
NT = (((1,), (1,)), ((), ()))


def copy_count(tiles):
    return tiles * 12 + 40


def kernel(
    tiles,
    emb,
    log_mass_in,
    sig,
    listing,
    early,
    late,
    xs,
    ys,
    d,
    dt,
    fates_1,
    fates_0,
    w_0,
    lists,
    log_mass,
    lm_src,
    lm_win,
    bias,
    x_norm,
    y_norm,
    h_row,
    hb,
    ub,
    row_send,
    row_recv,
    col_send,
    col_near,
    col_far,
    a_send,
    a_recv,
    b_send,
    b_recv,
    kept,
    early_own,
    send_sem,
    recv_sem,
    local_sem,
):
    c = lax.axis_index("cells")
    t = lax.axis_index("tiles")
    n = lax.axis_size("cells")
    rows = xs.shape[1]
    depth = xs.shape[2]
    q_rows = ys.shape[2]
    n_src = rows // BLOCK
    n_q = q_rows // BLOCK
    n_tgt = 3 * n_q
    scale = LOG2E / (EPS * depth)
    t_rows = pl.ds(pl.multiple_of(t * q_rows, q_rows), q_rows)

    counter = [0]
    sends = []

    def fresh():
        counter[0] += 1
        return counter[0] - 1

    def present(offset):
        return jnp.logical_and(c + offset >= 0, c + offset < n)

    def to_tile(src, dst, step):
        return to_peer(src, dst, lax.rem(t + step, tiles))

    def to_peer(src, dst, peer):
        i = fresh()
        copy = pltpu.make_async_remote_copy(
            src_ref=src,
            dst_ref=dst,
            send_sem=send_sem.at[i],
            recv_sem=recv_sem.at[i],
            device_id={"tiles": peer},
            device_id_type=pl.DeviceIdType.MESH,
        )
        copy.start()
        sends.append((copy, None))
        return copy.wait_recv

    def to_cell(src, dst, offset):
        i = fresh()
        copy = pltpu.make_async_remote_copy(
            src_ref=src,
            dst_ref=dst,
            send_sem=send_sem.at[i],
            recv_sem=recv_sem.at[i],
            device_id={"cells": c + offset},
            device_id_type=pl.DeviceIdType.MESH,
        )

        @pl.when(present(offset))
        def _():
            copy.start()

        sends.append((copy, offset))

        def wait():
            @pl.when(present(-offset))
            def _():
                copy.wait_recv()

        return wait

    for offset, part in ((1, 0), (-1, 2)):

        @pl.when(jnp.logical_not(present(-offset)))
        def _(part=part):
            for k in range(2):
                ys[k, part] = jnp.zeros(ys.shape[2:], BF16)
            fates_1[part] = jnp.zeros(fates_1.shape[1:], BF16)
            for f in range(2):
                fates_0[f, part] = jnp.zeros(fates_0.shape[2:], BF16)
            lm_win[part] = jnp.zeros(lm_win.shape[1:], F32)

    for buffer in (col_near, col_far):
        buffer[:, :, :, :, 0] = jnp.full(buffer.shape[:4] + buffer.shape[5:], NEG, F32)
        buffer[:, :, :, :, 1] = jnp.zeros(buffer.shape[:4] + buffer.shape[5:], F32)
    col_send[:, :, :, 0] = jnp.full(col_send.shape[:3] + col_send.shape[4:], NEG, F32)
    col_send[:, :, :, 1] = jnp.ones(col_send.shape[:3] + col_send.shape[4:], F32)

    barrier = pltpu.get_barrier_semaphore()
    for step in range(1, tiles):
        pl.semaphore_signal(
            barrier, inc=1, device_id={"tiles": lax.rem(t + step, tiles)}, device_id_type=pl.DeviceIdType.MESH
        )
    for offset in (1, -1, 2, -2):

        @pl.when(present(offset))
        def _(offset=offset):
            pl.semaphore_signal(
                barrier, inc=1, device_id={"cells": c + offset}, device_id_type=pl.DeviceIdType.MESH
            )

    local = []
    for i, (src, dst) in enumerate(
        (
            (emb.at[1], xs.at[1]),
            (emb.at[2, t_rows], ys.at[1, 1]),
            (emb.at[0], xs.at[0]),
            (emb.at[1, t_rows], ys.at[0, 1]),
            (sig.at[t_rows], fates_1.at[1]),
            (log_mass_in, log_mass),
            (listing, lists.at[0]),
        )
    ):
        copy = pltpu.make_async_copy(src, dst, local_sem.at[i])
        copy.start()
        local.append(copy)

    local[5].wait()
    lm_src[...] = jnp.zeros(lm_src.shape, F32)
    for k in range(2):
        for q in range(n_q):
            lanes = pl.ds(pl.multiple_of((t * n_q + q) * BLOCK, BLOCK), BLOCK)
            lm_src[k, q : q + 1, :] = log_mass[k + 1 : k + 2, lanes] * LOG2E
    lm_win[1] = lm_src[...]

    peers = sum(present(offset).astype(jnp.int32) for offset in (1, -1, 2, -2))
    pl.semaphore_wait(barrier, tiles - 1 + peers)

    list_waits = [to_tile(listing, lists.at[step], step) for step in range(1, tiles)]
    near = ((1, 0), (-1, 2))
    lm_waits = [to_cell(lm_src, lm_win.at[part], offset) for offset, part in near]
    y_waits = [None, None]
    y_waits[1] = [to_cell(emb.at[2, t_rows], ys.at[1, part], offset) for offset, part in near]

    local[6].wait()
    for wait in list_waits:
        wait()

    pair = lax.broadcasted_iota(jnp.int32, (n_src * n_tgt, 1), 0)
    src_id = c * n_src + pair // n_tgt
    slot = pair % n_tgt
    tgt_id = (c - 1 + slot // n_q) * n_src + t * n_q + slot % n_q
    for k in range(2):
        found = jnp.zeros((n_src * n_tgt, 1), F32)
        for step in range(tiles):
            hit = jnp.logical_and(
                lists[step, k, 0:1, :] == src_id, lists[step, k, 1:2, :] == tgt_id
            )
            found = found + jnp.sum(jnp.where(hit, 1.0, 0.0), axis=1, keepdims=True)
        bias[k] = jnp.broadcast_to(jnp.where(found > 0.0, 0.0, NEG), (n_src * n_tgt, BLOCK))

    def norm_row(block):
        wide = block.astype(F32)
        square = wide * wide
        folded = sum(square[:, e : e + BLOCK] for e in range(0, depth, BLOCK))
        return scale * jnp.sum(jnp.transpose(folded), axis=0, keepdims=True)

    def source_norms(k):
        @pl.loop(0, n_src)
        def _(b):
            x_norm[k, pl.ds(b, 1), :] = norm_row(xs[k, pl.ds(pl.multiple_of(b * BLOCK, BLOCK), BLOCK), :])

    def products(k, part):
        y = ys[k, part]
        for q in range(n_q):
            y_norm[k, part, q : q + 1, :] = norm_row(y[q * BLOCK : (q + 1) * BLOCK])

        @pl.loop(0, n_src // 2)
        def _(pair_index):
            x = xs[k, pl.ds(pl.multiple_of(pair_index * 2 * BLOCK, 2 * BLOCK), 2 * BLOCK), :]
            cross = lax.dot_general(x, y, NT, preferred_element_type=F32) * (2.0 * scale)
            crossed = lax.dot_general(y, x, NT, preferred_element_type=F32) * (2.0 * scale)
            for side in range(2):
                b = pair_index * 2 + side
                block = pl.ds(pl.multiple_of(b * BLOCK, BLOCK), BLOCK)
                own = slice(side * BLOCK, (side + 1) * BLOCK)
                for q in range(n_q):
                    j = part * n_q + q
                    shift = bias[k, pl.ds(b * n_tgt + j, 1), :]
                    other = slice(q * BLOCK, (q + 1) * BLOCK)
                    d[k, j, block, :] = cross[own, other] + shift
                    dt[k, b, j * BLOCK : (j + 1) * BLOCK, :] = crossed[other, own] + shift

    def fold(combine, slabs):
        value = functools.reduce(combine, slabs)
        while value.shape[0] > 1:
            middle = value.shape[0] // 2
            value = combine(value[:middle], value[middle:])
        return value

    def log_sum(terms, products_of, count):
        slabs = [
            (terms[b * BLOCK : (b + 1) * BLOCK, :] + products_of[b * BLOCK : (b + 1) * BLOCK, :]).reshape(
                BLOCK // 8, 8, BLOCK
            )
            for b in range(count)
        ]
        high = fold(jnp.maximum, slabs)
        mass = fold(jnp.add, [jnp.exp2(slab - high) for slab in slabs])[0]
        high = high[0]
        highest = jnp.max(high, axis=0, keepdims=True)
        return highest, jnp.sum(mass * jnp.exp2(high - highest), axis=0, keepdims=True)

    def down(row):
        return jnp.transpose(jnp.broadcast_to(row, (BLOCK, BLOCK)))

    def row_pass(k, phase):
        for j in range(n_tgt):
            hb[k, j * BLOCK : (j + 1) * BLOCK, :] = down(h_row[k, j // n_q, j % n_q : j % n_q + 1, :])

        @pl.loop(0, n_src // 2)
        def _(pair_index):
            for side in range(2):
                b = pair_index * 2 + side
                highest, mass = log_sum(hb.at[k], dt.at[k, b], n_tgt)
                row_send[k, phase, 0, pl.ds(b, 1), :] = highest
                row_send[k, phase, 1, pl.ds(b, 1), :] = mass

        return [
            to_tile(row_send.at[k, phase], row_recv.at[k, phase, step - 1], step) for step in range(1, tiles)
        ]

    def merged(pairs):
        highest = functools.reduce(jnp.maximum, [pair[0] for pair in pairs])
        total = sum(pair[1] * jnp.exp2(pair[0] - highest) for pair in pairs)
        return highest + jnp.log(total) * LOG2E

    def row_total(k, phase, waits):
        for wait in waits:
            wait()
        pairs = [(row_send[k, phase, 0], row_send[k, phase, 1])]
        pairs += [(row_recv[k, phase, s, 0], row_recv[k, phase, s, 1]) for s in range(tiles - 1)]
        return merged(pairs)

    def spread(k, values):
        for b in range(n_src):
            ub[k, b * BLOCK : (b + 1) * BLOCK, :] = down(values[b : b + 1])

    def col_pass(k, phase, total):
        mass = jnp.concatenate(
            [log_mass[k : k + 1, b * BLOCK : (b + 1) * BLOCK] for b in range(n_src)], axis=0
        )
        spread(k, mass * LOG2E - LAM * total + (LAM - 1.0) * x_norm[k])

        @pl.loop(0, 3)
        def _(part):
            for q in range(n_q):
                highest, mass = log_sum(ub.at[k], d.at[k, part * n_q + q], n_src)
                col_send[k, phase, part, 0, q : q + 1, :] = highest
                col_send[k, phase, part, 1, q : q + 1, :] = mass

        mine = col_send.at[k, phase]
        return [
            to_cell(mine.at[pl.ds(1, 2)], col_near.at[k, phase, 0], 1),
            to_cell(mine.at[pl.ds(0, 2)], col_near.at[k, phase, 1], -1),
            to_cell(mine.at[pl.ds(2, 1)], col_far.at[k, phase, 0], 2),
            to_cell(mine.at[pl.ds(0, 1)], col_far.at[k, phase, 1], -2),
        ]

    def col_total(k, phase, waits):
        for wait in waits:
            wait()

        def pair(ref):
            return ref[0], ref[1]

        mine = col_send.at[k, phase]
        below, above = col_near.at[k, phase, 0], col_near.at[k, phase, 1]
        far_below, far_above = col_far.at[k, phase, 0, 0], col_far.at[k, phase, 1, 0]
        totals = (
            merged([pair(far_below), pair(below.at[0]), pair(mine.at[0])]),
            merged([pair(below.at[1]), pair(mine.at[1]), pair(above.at[0])]),
            merged([pair(mine.at[2]), pair(above.at[1]), pair(far_above)]),
        )
        for part in range(3):
            h_row[k, part] = lm_win[part, k] - LAM * totals[part] + (LAM - 1.0) * y_norm[k, part]

    y_norm[...] = jnp.zeros(y_norm.shape, F32)
    local[0].wait()
    local[1].wait()
    source_norms(1)
    products(1, 1)
    local[2].wait()
    local[3].wait()
    source_norms(0)
    products(0, 1)
    for wait in lm_waits:
        wait()
    row_waits, col_waits = {}, {}
    for k in (1, 0):
        for wait in y_waits[k]:
            wait()
        if k == 1:
            y_waits[0] = [to_cell(emb.at[1, t_rows], ys.at[0, part], offset) for offset, part in near]
        else:
            sig_waits = [to_cell(sig.at[t_rows], fates_1.at[part], offset) for offset, part in near]
        for _, part in near:
            products(k, part)
        for part in range(3):
            h_row[k, part] = lm_win[part, k] - y_norm[k, part]
        row_waits[k] = row_pass(k, 0)
    for sweep in range(SWEEPS):
        for k in (1, 0):
            col_waits[k] = col_pass(k, sweep, row_total(k, sweep, row_waits[k]))
        for k in (1, 0):
            col_total(k, sweep, col_waits[k])
            row_waits[k] = row_pass(k, sweep + 1)

    def weights(k, block, part):
        return jnp.concatenate(
            [
                jnp.exp2(
                    h_row[k, part, q : q + 1, :] + d[k, part * n_q + q, block, :] - ub[k, block, :]
                ).astype(BF16)
                for q in range(n_q)
            ],
            axis=1,
        )

    def row_block(index):
        return pl.ds(pl.multiple_of(index * q_rows, q_rows), q_rows)

    spread(1, row_total(1, SWEEPS, row_waits[1]))
    local[4].wait()
    for wait in sig_waits:
        wait()
    t_1 = t + 1 - 2 * lax.rem(t, 2)
    t_2 = lax.rem(t + 2, tiles)
    t_3 = lax.rem(t_1 + 2, tiles)
    half = fates_0.shape[3]
    lanes = [slice(f * half, (f + 1) * half) for f in range(2)]

    def late_part(index):
        block = row_block(index)
        return sum(
            jnp.dot(weights(1, block, part), fates_1[part], preferred_element_type=F32) for part in range(3)
        )

    def early_part(index, f):
        block = row_block(index)
        return sum(
            jnp.dot(w_0[part, block, :], fates_0[f, part], preferred_element_type=F32) for part in range(3)
        )

    def to_mate(k, f):
        return to_peer(a_send.at[k, f], a_recv.at[k, f], t_1)

    def across(k, f, arrived):
        arrived()
        b_send[k, f] = (kept[k, f, 1] + a_recv[k, f, 1].astype(F32)).astype(BF16)
        return to_peer(b_send.at[k, f], b_recv.at[k, f], t_2)

    def summed(k, f, arrived):
        arrived()
        return (kept[k, f, 0] + a_recv[k, f, 0].astype(F32) + b_recv[k, f].astype(F32)).astype(BF16)

    def gather(block, out, f):
        here = out.at[t_rows, lanes[f]]
        return to_peer(block, here, t_1), to_peer(block, here, t_2)

    def forward(waits, out, f):
        waits[1]()
        there = out.at[row_block(t_2), lanes[f]]
        return [waits[0], to_peer(there, there, t_1)]

    for i, index in enumerate((t_1, t_3)):
        total = late_part(index)
        for f in range(2):
            a_send[1, f, i] = total[:, lanes[f]].astype(BF16)
    a_waits = [to_mate(1, f) for f in range(2)]
    for i, index in enumerate((t, t_2)):
        total = late_part(index)
        for f in range(2):
            kept[1, f, i] = total[:, lanes[f]]
    b_waits = [across(1, f, a_waits[f]) for f in range(2)]

    spread(0, row_total(0, SWEEPS, row_waits[0]))

    @pl.loop(0, tiles)
    def _(r):
        block = row_block(r)
        for part in range(3):
            w_0[part, block, :] = weights(0, block, part)

    late_waits, late_gather = [], []
    for f in range(2):
        fates_0[f, 1] = summed(1, f, b_waits[f])
        late_waits.append([to_cell(fates_0.at[f, 1], fates_0.at[f, part], offset) for offset, part in near])
        late_gather.append(gather(fates_0.at[f, 1], late, f))
        late[t_rows, lanes[f]] = fates_0[f, 1]

    b_waits = []
    for f in range(2):
        for wait in late_waits[f]:
            wait()
        for i, index in enumerate((t_1, t_3)):
            a_send[0, f, i] = early_part(index, f).astype(BF16)
        arrived = to_mate(0, f)
        for i, index in enumerate((t, t_2)):
            kept[0, f, i] = early_part(index, f)
        b_waits.append(across(0, f, arrived))
    gather_waits = []
    for f in range(2):
        gather_waits += forward(late_gather[f], late, f)
    early_gather = []
    for f in range(2):
        early_own[f] = summed(0, f, b_waits[f])
        early_gather.append(gather(early_own.at[f], early, f))
        early[t_rows, lanes[f]] = early_own[f]
    for f in range(2):
        gather_waits += forward(early_gather[f], early, f)
    for wait in gather_waits:
        wait()
    for copy, offset in sends:
        if offset is None:
            copy.wait_send()
        else:

            @pl.when(present(offset))
            def _(copy=copy):
                copy.wait_send()


def on_device(tiles, embeddings, log_mass, signatures, tile_list):
    _, rows, depth = embeddings.shape
    fate = signatures.shape[1]
    q_rows = rows // tiles
    n_src = rows // BLOCK
    n_q = q_rows // BLOCK
    n_tgt = 3 * n_q
    vmem = pltpu.VMEM
    copies = copy_count(tiles)
    return pl.pallas_call(
        functools.partial(kernel, tiles),
        out_shape=(
            jax.ShapeDtypeStruct((rows, fate), BF16),
            jax.ShapeDtypeStruct((rows, fate), BF16),
        ),
        in_specs=[pl.BlockSpec(memory_space=pltpu.HBM)] * 4,
        out_specs=(pl.BlockSpec(memory_space=vmem), pl.BlockSpec(memory_space=vmem)),
        scratch_shapes=[
            vmem((2, rows, depth), BF16),
            vmem((2, 3, q_rows, depth), BF16),
            vmem((2, n_tgt, rows, BLOCK), F32),
            vmem((2, n_src, n_tgt * BLOCK, BLOCK), F32),
            vmem((3, q_rows, fate), BF16),
            vmem((2, 3, q_rows, fate // 2), BF16),
            vmem((3, rows, q_rows), BF16),
            vmem((tiles,) + tile_list.shape, jnp.int32),
            vmem(log_mass.shape, F32),
            vmem((2, 8, BLOCK), F32),
            vmem((3, 2, 8, BLOCK), F32),
            vmem((2, n_src * n_tgt, BLOCK), F32),
            vmem((2, n_src, BLOCK), F32),
            vmem((2, 3, 8, BLOCK), F32),
            vmem((2, 3, 8, BLOCK), F32),
            vmem((2, n_tgt * BLOCK, BLOCK), F32),
            vmem((2, rows, BLOCK), F32),
            vmem((2, SWEEPS + 1, 2, n_src, BLOCK), F32),
            vmem((2, SWEEPS + 1, tiles - 1, 2, n_src, BLOCK), F32),
            vmem((2, SWEEPS, 3, 2, 8, BLOCK), F32),
            vmem((2, SWEEPS, 2, 2, 2, 8, BLOCK), F32),
            vmem((2, SWEEPS, 2, 1, 2, 8, BLOCK), F32),
            vmem((2, 2, 2, q_rows, fate // 2), BF16),
            vmem((2, 2, 2, q_rows, fate // 2), BF16),
            vmem((2, 2, q_rows, fate // 2), BF16),
            vmem((2, 2, q_rows, fate // 2), BF16),
            vmem((2, 2, 2, q_rows, fate // 2), F32),
            vmem((2, q_rows, fate // 2), BF16),
            pltpu.SemaphoreType.DMA((copies,)),
            pltpu.SemaphoreType.DMA((copies,)),
            pltpu.SemaphoreType.DMA((7,)),
        ],
        compiler_params=pltpu.CompilerParams(
            collective_id=0, has_side_effects=True, vmem_limit_bytes=58 * 1024 * 1024
        ),
    )(embeddings, log_mass, signatures, tile_list)


def solution(mesh):
    in_specs = (
        P(None, "cells", None),
        P(None, "cells"),
        P("cells", None),
        P(None, None, ("cells", "tiles")),
    )
    out_specs = (P("cells", None), P("cells", None))
    return jax.shard_map(
        functools.partial(on_device, mesh.shape["tiles"]),
        mesh=mesh,
        in_specs=in_specs,
        out_specs=out_specs,
        check_vma=False,
    )
```

```python
import functools
import math

import jax
import jax.numpy as jnp
from jax import lax
from jax.experimental import pallas as pl
from jax.experimental.pallas import tpu as pltpu
from jax.sharding import PartitionSpec as P

BLOCK = 128
SWEEPS = 2
EPS = 0.01
RHO = 1.0
NEG = -1e30
LOG2E = math.log2(math.e)
LAM = RHO / (RHO + EPS)
F32 = jnp.float32
BF16 = jnp.bfloat16
NT = (((1,), (1,)), ((), ()))


def copy_count(tiles):
    return tiles * 12 + 48


def kernel(
    tiles,
    emb,
    log_mass_in,
    sig,
    listing,
    early,
    late,
    xs,
    ys,
    d,
    dt,
    fates_1,
    fates_0,
    w_0,
    lists,
    log_mass,
    lm_src,
    lm_win,
    bias,
    x_norm,
    y_norm,
    h_row,
    hb,
    ub,
    row_send,
    row_recv,
    col_send,
    col_near,
    col_far,
    a_send,
    a_recv,
    b_send,
    b_recv,
    kept,
    early_own,
    send_sem,
    recv_sem,
    local_sem,
):
    c = lax.axis_index("cells")
    t = lax.axis_index("tiles")
    n = lax.axis_size("cells")
    rows = xs.shape[1]
    depth = xs.shape[2]
    q_rows = ys.shape[2]
    n_src = rows // BLOCK
    n_q = q_rows // BLOCK
    n_tgt = 3 * n_q
    scale = LOG2E / (EPS * depth)
    t_rows = pl.ds(pl.multiple_of(t * q_rows, q_rows), q_rows)

    counter = [0]
    sends = []

    def fresh():
        counter[0] += 1
        return counter[0] - 1

    def present(offset):
        return jnp.logical_and(c + offset >= 0, c + offset < n)

    def to_tile(src, dst, step):
        return to_peer(src, dst, lax.rem(t + step, tiles))

    def to_peer(src, dst, peer):
        i = fresh()
        copy = pltpu.make_async_remote_copy(
            src_ref=src,
            dst_ref=dst,
            send_sem=send_sem.at[i],
            recv_sem=recv_sem.at[i],
            device_id={"tiles": peer},
            device_id_type=pl.DeviceIdType.MESH,
        )
        copy.start()
        sends.append((copy, None))
        return copy.wait_recv

    def to_cell(src, dst, offset, origin=None):
        origin = -offset if origin is None else origin
        i = fresh()
        copy = pltpu.make_async_remote_copy(
            src_ref=src,
            dst_ref=dst,
            send_sem=send_sem.at[i],
            recv_sem=recv_sem.at[i],
            device_id={"cells": c + offset},
            device_id_type=pl.DeviceIdType.MESH,
        )

        @pl.when(present(offset))
        def _():
            copy.start()

        sends.append((copy, offset))

        def wait():
            @pl.when(present(origin))
            def _():
                copy.wait_recv()

        return wait

    for offset, part in ((1, 0), (-1, 2)):

        @pl.when(jnp.logical_not(present(-offset)))
        def _(part=part):
            for k in range(2):
                ys[k, part] = jnp.zeros(ys.shape[2:], BF16)
            fates_1[part] = jnp.zeros(fates_1.shape[1:], BF16)
            for f in range(2):
                fates_0[f, part] = jnp.zeros(fates_0.shape[2:], BF16)
            lm_win[part] = jnp.zeros(lm_win.shape[1:], F32)

    for buffer in (col_near, col_far):
        buffer[:, :, :, :, 0] = jnp.full(buffer.shape[:4] + buffer.shape[5:], NEG, F32)
        buffer[:, :, :, :, 1] = jnp.zeros(buffer.shape[:4] + buffer.shape[5:], F32)
    col_send[:, :, :, 0] = jnp.full(col_send.shape[:3] + col_send.shape[4:], NEG, F32)
    col_send[:, :, :, 1] = jnp.ones(col_send.shape[:3] + col_send.shape[4:], F32)

    barrier = pltpu.get_barrier_semaphore()
    for step in range(1, tiles):
        pl.semaphore_signal(
            barrier, inc=1, device_id={"tiles": lax.rem(t + step, tiles)}, device_id_type=pl.DeviceIdType.MESH
        )
    for offset in (1, -1, 2, -2):

        @pl.when(present(offset))
        def _(offset=offset):
            pl.semaphore_signal(
                barrier, inc=1, device_id={"cells": c + offset}, device_id_type=pl.DeviceIdType.MESH
            )

    local = []
    for i, (src, dst) in enumerate(
        (
            (emb.at[1], xs.at[1]),
            (emb.at[2, t_rows], ys.at[1, 1]),
            (emb.at[0], xs.at[0]),
            (emb.at[1, t_rows], ys.at[0, 1]),
            (sig.at[t_rows], fates_1.at[1]),
            (log_mass_in, log_mass),
            (listing, lists.at[0]),
        )
    ):
        copy = pltpu.make_async_copy(src, dst, local_sem.at[i])
        copy.start()
        local.append(copy)

    local[5].wait()
    lm_src[...] = jnp.zeros(lm_src.shape, F32)
    for k in range(2):
        for q in range(n_q):
            lanes = pl.ds(pl.multiple_of((t * n_q + q) * BLOCK, BLOCK), BLOCK)
            lm_src[k, q : q + 1, :] = log_mass[k + 1 : k + 2, lanes] * LOG2E
    lm_win[1] = lm_src[...]

    peers = sum(present(offset).astype(jnp.int32) for offset in (1, -1, 2, -2))
    pl.semaphore_wait(barrier, tiles - 1 + peers)

    list_waits = [to_tile(listing, lists.at[step], step) for step in range(1, tiles)]
    near = ((1, 0), (-1, 2))
    lm_waits = [to_cell(lm_src, lm_win.at[part], offset) for offset, part in near]

    odd = lax.rem(c, 2)
    mate = 1 - 2 * odd
    part_in, part_out = 2 - 2 * odd, 2 * odd

    def to_pair(pieces):
        return [(to_cell(src, buffer.at[part_out], mate, mate), buffer) for src, buffer in pieces]

    def hand_on(arrivals):
        waits = []
        for arrived, buffer in arrivals:
            arrived()
            waits.append(to_cell(buffer.at[part_in], buffer.at[part_out], 2 * mate))
        return waits

    def embedding_pieces(k):
        pieces = []
        for q in range(n_q):
            start = pl.multiple_of(t * q_rows + q * BLOCK, BLOCK)
            pieces.append((emb.at[k + 1, pl.ds(start, BLOCK)], ys.at[k, :, pl.ds(q * BLOCK, BLOCK)]))
        return pieces

    y_arrivals = to_pair(embedding_pieces(1))

    local[6].wait()
    for wait in list_waits:
        wait()

    pair = lax.broadcasted_iota(jnp.int32, (n_src * n_tgt, 1), 0)
    src_id = c * n_src + pair // n_tgt
    slot = pair % n_tgt
    tgt_id = (c - 1 + slot // n_q) * n_src + t * n_q + slot % n_q
    for k in range(2):
        found = jnp.zeros((n_src * n_tgt, 1), F32)
        for step in range(tiles):
            hit = jnp.logical_and(
                lists[step, k, 0:1, :] == src_id, lists[step, k, 1:2, :] == tgt_id
            )
            found = found + jnp.sum(jnp.where(hit, 1.0, 0.0), axis=1, keepdims=True)
        bias[k] = jnp.broadcast_to(jnp.where(found > 0.0, 0.0, NEG), (n_src * n_tgt, BLOCK))

    def norm_row(block):
        wide = block.astype(F32)
        square = wide * wide
        folded = sum(square[:, e : e + BLOCK] for e in range(0, depth, BLOCK))
        return scale * jnp.sum(jnp.transpose(folded), axis=0, keepdims=True)

    def source_norms(k):
        @pl.loop(0, n_src)
        def _(b):
            x_norm[k, pl.ds(b, 1), :] = norm_row(xs[k, pl.ds(pl.multiple_of(b * BLOCK, BLOCK), BLOCK), :])

    def products(k, part):
        y = ys[k, part]
        for q in range(n_q):
            y_norm[k, part, q : q + 1, :] = norm_row(y[q * BLOCK : (q + 1) * BLOCK])

        @pl.loop(0, n_src // 2)
        def _(pair_index):
            x = xs[k, pl.ds(pl.multiple_of(pair_index * 2 * BLOCK, 2 * BLOCK), 2 * BLOCK), :]
            cross = lax.dot_general(x, y, NT, preferred_element_type=F32) * (2.0 * scale)
            crossed = lax.dot_general(y, x, NT, preferred_element_type=F32) * (2.0 * scale)
            for side in range(2):
                b = pair_index * 2 + side
                block = pl.ds(pl.multiple_of(b * BLOCK, BLOCK), BLOCK)
                own = slice(side * BLOCK, (side + 1) * BLOCK)
                for q in range(n_q):
                    j = part * n_q + q
                    shift = bias[k, pl.ds(b * n_tgt + j, 1), :]
                    other = slice(q * BLOCK, (q + 1) * BLOCK)
                    d[k, j, block, :] = cross[own, other] + shift
                    dt[k, b, pl.ds(pl.multiple_of(j * BLOCK, BLOCK), BLOCK), :] = crossed[other, own] + shift

    def fold(combine, slabs):
        value = functools.reduce(combine, slabs)
        while value.shape[0] > 1:
            middle = value.shape[0] // 2
            value = combine(value[:middle], value[middle:])
        return value

    def log_sum(terms, products_of, count):
        slabs = [
            (terms[b * BLOCK : (b + 1) * BLOCK, :] + products_of[b * BLOCK : (b + 1) * BLOCK, :]).reshape(
                BLOCK // 8, 8, BLOCK
            )
            for b in range(count)
        ]
        high = fold(jnp.maximum, slabs)
        mass = fold(jnp.add, [jnp.exp2(slab - high) for slab in slabs])[0]
        high = high[0]
        highest = jnp.max(high, axis=0, keepdims=True)
        return highest, jnp.sum(mass * jnp.exp2(high - highest), axis=0, keepdims=True)

    def down(row):
        return jnp.transpose(jnp.broadcast_to(row, (BLOCK, BLOCK)))

    def row_pass(k, phase):
        for j in range(n_tgt):
            hb[k, j * BLOCK : (j + 1) * BLOCK, :] = down(h_row[k, j // n_q, j % n_q : j % n_q + 1, :])

        @pl.loop(0, n_src // 2)
        def _(pair_index):
            for side in range(2):
                b = pair_index * 2 + side
                highest, mass = log_sum(hb.at[k], dt.at[k, b], n_tgt)
                row_send[k, phase, 0, pl.ds(b, 1), :] = highest
                row_send[k, phase, 1, pl.ds(b, 1), :] = mass

        return [
            to_tile(row_send.at[k, phase], row_recv.at[k, phase, step - 1], step) for step in range(1, tiles)
        ]

    def merged(pairs):
        highest = functools.reduce(jnp.maximum, [pair[0] for pair in pairs])
        total = sum(pair[1] * jnp.exp2(pair[0] - highest) for pair in pairs)
        return highest + jnp.log(total) * LOG2E

    def row_total(k, phase, waits):
        for wait in waits:
            wait()
        pairs = [(row_send[k, phase, 0], row_send[k, phase, 1])]
        pairs += [(row_recv[k, phase, s, 0], row_recv[k, phase, s, 1]) for s in range(tiles - 1)]
        return merged(pairs)

    def spread(k, values):
        for b in range(n_src):
            ub[k, b * BLOCK : (b + 1) * BLOCK, :] = down(values[b : b + 1])

    def col_pass(k, phase, total):
        mass = jnp.concatenate(
            [log_mass[k : k + 1, b * BLOCK : (b + 1) * BLOCK] for b in range(n_src)], axis=0
        )
        spread(k, mass * LOG2E - LAM * total + (LAM - 1.0) * x_norm[k])

        @pl.loop(0, 3)
        def _(part):
            for q in range(n_q):
                highest, mass = log_sum(ub.at[k], d.at[k, part * n_q + q], n_src)
                col_send[k, phase, part, 0, q : q + 1, :] = highest
                col_send[k, phase, part, 1, q : q + 1, :] = mass

        mine = col_send.at[k, phase]
        return [
            to_cell(mine.at[pl.ds(1, 2)], col_near.at[k, phase, 0], 1),
            to_cell(mine.at[pl.ds(0, 2)], col_near.at[k, phase, 1], -1),
            to_cell(mine.at[pl.ds(2, 1)], col_far.at[k, phase, 0], 2),
            to_cell(mine.at[pl.ds(0, 1)], col_far.at[k, phase, 1], -2),
        ]

    def col_total(k, phase, waits):
        for wait in waits:
            wait()

        def pair(ref):
            return ref[0], ref[1]

        mine = col_send.at[k, phase]
        below, above = col_near.at[k, phase, 0], col_near.at[k, phase, 1]
        far_below, far_above = col_far.at[k, phase, 0, 0], col_far.at[k, phase, 1, 0]
        totals = (
            merged([pair(far_below), pair(below.at[0]), pair(mine.at[0])]),
            merged([pair(below.at[1]), pair(mine.at[1]), pair(above.at[0])]),
            merged([pair(mine.at[2]), pair(above.at[1]), pair(far_above)]),
        )
        for part in range(3):
            h_row[k, part] = lm_win[part, k] - LAM * totals[part] + (LAM - 1.0) * y_norm[k, part]

    y_norm[...] = jnp.zeros(y_norm.shape, F32)
    local[0].wait()
    local[1].wait()
    source_norms(1)
    products(1, 1)
    local[2].wait()
    local[3].wait()
    source_norms(0)
    products(0, 1)
    for wait in lm_waits:
        wait()
    row_waits, col_waits = {}, {}

    def first_rows(k, y_waits):
        products(k, part_in)
        for wait in y_waits:
            wait()
        products(k, part_out)
        for part in range(3):
            h_row[k, part] = lm_win[part, k] - y_norm[k, part]
        row_waits[k] = row_pass(k, 0)

    def columns(k, sweep):
        col_waits[k] = col_pass(k, sweep, row_total(k, sweep, row_waits[k]))

    def next_rows(k, sweep):
        col_total(k, sweep, col_waits[k])
        row_waits[k] = row_pass(k, sweep + 1)

    y_waits = hand_on(y_arrivals)
    y_arrivals = to_pair(embedding_pieces(0))
    first_rows(1, y_waits)
    y_waits = hand_on(y_arrivals)
    sig_arrivals = to_pair([(sig.at[t_rows], fates_1)])
    columns(1, 0)
    first_rows(0, y_waits)
    sig_waits = hand_on(sig_arrivals)
    for sweep in range(SWEEPS):
        next_rows(1, sweep)
        columns(0, sweep)
        if sweep + 1 < SWEEPS:
            columns(1, sweep + 1)
            next_rows(0, sweep)

    def weights(k, block, part):
        return jnp.concatenate(
            [
                jnp.exp2(
                    h_row[k, part, q : q + 1, :] + d[k, part * n_q + q, block, :] - ub[k, block, :]
                ).astype(BF16)
                for q in range(n_q)
            ],
            axis=1,
        )

    def row_block(index):
        return pl.ds(pl.multiple_of(index * q_rows, q_rows), q_rows)

    spread(1, row_total(1, SWEEPS, row_waits[1]))
    local[4].wait()
    for wait in sig_waits:
        wait()
    t_1 = t + 1 - 2 * lax.rem(t, 2)
    t_2 = lax.rem(t + 2, tiles)
    t_3 = lax.rem(t_1 + 2, tiles)
    half = fates_0.shape[3]
    lanes = [slice(f * half, (f + 1) * half) for f in range(2)]

    def late_part(index):
        block = row_block(index)
        return sum(
            jnp.dot(weights(1, block, part), fates_1[part], preferred_element_type=F32) for part in range(3)
        )

    def early_part(index, f):
        block = row_block(index)
        return sum(
            jnp.dot(w_0[part, block, :], fates_0[f, part], preferred_element_type=F32) for part in range(3)
        )

    def to_mate(k, f):
        return to_peer(a_send.at[k, f], a_recv.at[k, f], t_1)

    def across(k, f, arrived):
        arrived()
        b_send[k, f] = (kept[k, f, 1] + a_recv[k, f, 1].astype(F32)).astype(BF16)
        return to_peer(b_send.at[k, f], b_recv.at[k, f], t_2)

    def summed(k, f, arrived):
        arrived()
        return (kept[k, f, 0] + a_recv[k, f, 0].astype(F32) + b_recv[k, f].astype(F32)).astype(BF16)

    def gather(block, out, f):
        here = out.at[t_rows, lanes[f]]
        return to_peer(block, here, t_1), to_peer(block, here, t_2)

    def forward(waits, out, f):
        waits[1]()
        there = out.at[row_block(t_2), lanes[f]]
        return [waits[0], to_peer(there, there, t_1)]

    for i, index in enumerate((t_1, t_3)):
        total = late_part(index)
        for f in range(2):
            a_send[1, f, i] = total[:, lanes[f]].astype(BF16)
    a_waits = [to_mate(1, f) for f in range(2)]
    for i, index in enumerate((t, t_2)):
        total = late_part(index)
        for f in range(2):
            kept[1, f, i] = total[:, lanes[f]]
    b_waits = [across(1, f, a_waits[f]) for f in range(2)]

    next_rows(0, SWEEPS - 1)

    late_arrivals, late_gather = [], []
    for f in range(2):
        fates_0[f, 1] = summed(1, f, b_waits[f])
        late_arrivals.append(to_pair([(fates_0.at[f, 1], fates_0.at[f])]))
        late_gather.append(gather(fates_0.at[f, 1], late, f))
        late[t_rows, lanes[f]] = fates_0[f, 1]

    spread(0, row_total(0, SWEEPS, row_waits[0]))
    late_waits = [hand_on(late_arrivals[f]) for f in range(2)]

    @pl.loop(0, tiles)
    def _(r):
        block = row_block(r)
        for part in range(3):
            w_0[part, block, :] = weights(0, block, part)

    b_waits = []
    for f in range(2):
        for wait in late_waits[f]:
            wait()
        for i, index in enumerate((t_1, t_3)):
            a_send[0, f, i] = early_part(index, f).astype(BF16)
        arrived = to_mate(0, f)
        for i, index in enumerate((t, t_2)):
            kept[0, f, i] = early_part(index, f)
        b_waits.append(across(0, f, arrived))
    gather_waits = []
    for f in range(2):
        gather_waits += forward(late_gather[f], late, f)
    early_gather = []
    for f in range(2):
        early_own[f] = summed(0, f, b_waits[f])
        early_gather.append(gather(early_own.at[f], early, f))
        early[t_rows, lanes[f]] = early_own[f]
    for f in range(2):
        gather_waits += forward(early_gather[f], early, f)
    for wait in gather_waits:
        wait()
    for copy, offset in sends:
        if offset is None:
            copy.wait_send()
        else:

            @pl.when(present(offset))
            def _(copy=copy):
                copy.wait_send()


def on_device(tiles, embeddings, log_mass, signatures, tile_list):
    _, rows, depth = embeddings.shape
    fate = signatures.shape[1]
    q_rows = rows // tiles
    n_src = rows // BLOCK
    n_q = q_rows // BLOCK
    n_tgt = 3 * n_q
    vmem = pltpu.VMEM
    copies = copy_count(tiles)
    return pl.pallas_call(
        functools.partial(kernel, tiles),
        out_shape=(
            jax.ShapeDtypeStruct((rows, fate), BF16),
            jax.ShapeDtypeStruct((rows, fate), BF16),
        ),
        in_specs=[pl.BlockSpec(memory_space=pltpu.HBM)] * 4,
        out_specs=(pl.BlockSpec(memory_space=vmem), pl.BlockSpec(memory_space=vmem)),
        scratch_shapes=[
            vmem((2, rows, depth), BF16),
            vmem((2, 3, q_rows, depth), BF16),
            vmem((2, n_tgt, rows, BLOCK), F32),
            vmem((2, n_src, n_tgt * BLOCK, BLOCK), F32),
            vmem((3, q_rows, fate), BF16),
            vmem((2, 3, q_rows, fate // 2), BF16),
            vmem((3, rows, q_rows), BF16),
            vmem((tiles,) + tile_list.shape, jnp.int32),
            vmem(log_mass.shape, F32),
            vmem((2, 8, BLOCK), F32),
            vmem((3, 2, 8, BLOCK), F32),
            vmem((2, n_src * n_tgt, BLOCK), F32),
            vmem((2, n_src, BLOCK), F32),
            vmem((2, 3, 8, BLOCK), F32),
            vmem((2, 3, 8, BLOCK), F32),
            vmem((2, n_tgt * BLOCK, BLOCK), F32),
            vmem((2, rows, BLOCK), F32),
            vmem((2, SWEEPS + 1, 2, n_src, BLOCK), F32),
            vmem((2, SWEEPS + 1, tiles - 1, 2, n_src, BLOCK), F32),
            vmem((2, SWEEPS, 3, 2, 8, BLOCK), F32),
            vmem((2, SWEEPS, 2, 2, 2, 8, BLOCK), F32),
            vmem((2, SWEEPS, 2, 1, 2, 8, BLOCK), F32),
            vmem((2, 2, 2, q_rows, fate // 2), BF16),
            vmem((2, 2, 2, q_rows, fate // 2), BF16),
            vmem((2, 2, q_rows, fate // 2), BF16),
            vmem((2, 2, q_rows, fate // 2), BF16),
            vmem((2, 2, 2, q_rows, fate // 2), F32),
            vmem((2, q_rows, fate // 2), BF16),
            pltpu.SemaphoreType.DMA((copies,)),
            pltpu.SemaphoreType.DMA((copies,)),
            pltpu.SemaphoreType.DMA((7,)),
        ],
        compiler_params=pltpu.CompilerParams(
            collective_id=0, has_side_effects=True, vmem_limit_bytes=58 * 1024 * 1024
        ),
    )(embeddings, log_mass, signatures, tile_list)


def solution(mesh):
    in_specs = (
        P(None, "cells", None),
        P(None, "cells"),
        P("cells", None),
        P(None, None, ("cells", "tiles")),
    )
    out_specs = (P("cells", None), P("cells", None))
    return jax.shard_map(
        functools.partial(on_device, mesh.shape["tiles"]),
        mesh=mesh,
        in_specs=in_specs,
        out_specs=out_specs,
        check_vma=False,
    )
```

```python
import functools
import math

import jax
import jax.numpy as jnp
from jax import lax
from jax.experimental import pallas as pl
from jax.experimental.pallas import tpu as pltpu
from jax.sharding import PartitionSpec as P

BLOCK = 128
SWEEPS = 2
EPS = 0.01
RHO = 1.0
NEG = -1e30
LOG2E = math.log2(math.e)
LAM = RHO / (RHO + EPS)
F32 = jnp.float32
BF16 = jnp.bfloat16
NT = (((1,), (1,)), ((), ()))


def copy_count(tiles):
    return tiles * 12 + 48


def kernel(
    tiles,
    emb,
    log_mass_in,
    sig,
    listing,
    early,
    late,
    xs,
    ys,
    d,
    dt,
    fates_1,
    fates_0,
    w_0,
    lists,
    log_mass,
    lm_src,
    lm_win,
    bias,
    x_norm,
    y_norm,
    h_row,
    hb,
    ub,
    row_send,
    row_recv,
    col_send,
    col_near,
    col_far,
    a_send,
    a_recv,
    b_send,
    b_recv,
    kept,
    early_own,
    send_sem,
    recv_sem,
    local_sem,
):
    c = lax.axis_index("cells")
    t = lax.axis_index("tiles")
    n = lax.axis_size("cells")
    rows = xs.shape[1]
    depth = xs.shape[2]
    q_rows = ys.shape[2]
    n_src = rows // BLOCK
    n_q = q_rows // BLOCK
    n_tgt = 3 * n_q
    scale = LOG2E / (EPS * depth)
    t_rows = pl.ds(pl.multiple_of(t * q_rows, q_rows), q_rows)

    counter = [0]
    sends = []

    def fresh():
        counter[0] += 1
        return counter[0] - 1

    def present(offset):
        return jnp.logical_and(c + offset >= 0, c + offset < n)

    def to_tile(src, dst, step):
        return to_peer(src, dst, lax.rem(t + step, tiles))

    def to_peer(src, dst, peer):
        i = fresh()
        copy = pltpu.make_async_remote_copy(
            src_ref=src,
            dst_ref=dst,
            send_sem=send_sem.at[i],
            recv_sem=recv_sem.at[i],
            device_id={"tiles": peer},
            device_id_type=pl.DeviceIdType.MESH,
        )
        copy.start()
        sends.append((copy, None))
        return copy.wait_recv

    def to_cell(src, dst, offset, origin=None):
        origin = -offset if origin is None else origin
        i = fresh()
        copy = pltpu.make_async_remote_copy(
            src_ref=src,
            dst_ref=dst,
            send_sem=send_sem.at[i],
            recv_sem=recv_sem.at[i],
            device_id={"cells": c + offset},
            device_id_type=pl.DeviceIdType.MESH,
        )

        @pl.when(present(offset))
        def _():
            copy.start()

        sends.append((copy, offset))

        def wait():
            @pl.when(present(origin))
            def _():
                copy.wait_recv()

        return wait

    for offset, part in ((1, 0), (-1, 2)):

        @pl.when(jnp.logical_not(present(-offset)))
        def _(part=part):
            for k in range(2):
                ys[k, part] = jnp.zeros(ys.shape[2:], BF16)
            fates_1[part] = jnp.zeros(fates_1.shape[1:], BF16)
            for f in range(2):
                fates_0[f, part] = jnp.zeros(fates_0.shape[2:], BF16)
            lm_win[part] = jnp.zeros(lm_win.shape[1:], F32)

    for buffer in (col_near, col_far):
        buffer[:, :, :, :, 0] = jnp.full(buffer.shape[:4] + buffer.shape[5:], NEG, F32)
        buffer[:, :, :, :, 1] = jnp.zeros(buffer.shape[:4] + buffer.shape[5:], F32)
    col_send[:, :, :, 0] = jnp.full(col_send.shape[:3] + col_send.shape[4:], NEG, F32)
    col_send[:, :, :, 1] = jnp.ones(col_send.shape[:3] + col_send.shape[4:], F32)

    barrier = pltpu.get_barrier_semaphore()
    for step in range(1, tiles):
        pl.semaphore_signal(
            barrier, inc=1, device_id={"tiles": lax.rem(t + step, tiles)}, device_id_type=pl.DeviceIdType.MESH
        )
    for offset in (1, -1, 2, -2):

        @pl.when(present(offset))
        def _(offset=offset):
            pl.semaphore_signal(
                barrier, inc=1, device_id={"cells": c + offset}, device_id_type=pl.DeviceIdType.MESH
            )

    local = []
    for i, (src, dst) in enumerate(
        (
            (emb.at[1], xs.at[1]),
            (emb.at[2, t_rows], ys.at[1, 1]),
            (emb.at[0], xs.at[0]),
            (emb.at[1, t_rows], ys.at[0, 1]),
            (sig.at[t_rows], fates_1.at[1]),
            (log_mass_in, log_mass),
            (listing, lists.at[0]),
        )
    ):
        copy = pltpu.make_async_copy(src, dst, local_sem.at[i])
        copy.start()
        local.append(copy)

    local[5].wait()
    lm_src[...] = jnp.zeros(lm_src.shape, F32)
    for k in range(2):
        for q in range(n_q):
            lanes = pl.ds(pl.multiple_of((t * n_q + q) * BLOCK, BLOCK), BLOCK)
            lm_src[k, q : q + 1, :] = log_mass[k + 1 : k + 2, lanes] * LOG2E
    lm_win[1] = lm_src[...]

    peers = sum(present(offset).astype(jnp.int32) for offset in (1, -1, 2, -2))
    pl.semaphore_wait(barrier, tiles - 1 + peers)

    list_waits = [to_tile(listing, lists.at[step], step) for step in range(1, tiles)]
    near = ((1, 0), (-1, 2))
    lm_waits = [to_cell(lm_src, lm_win.at[part], offset) for offset, part in near]

    odd = lax.rem(c, 2)
    mate = 1 - 2 * odd
    part_in, part_out = 2 - 2 * odd, 2 * odd

    def to_pair(pieces):
        return [(to_cell(src, buffer.at[part_out], mate, mate), buffer) for src, buffer in pieces]

    def hand_on(arrivals):
        waits = []
        for arrived, buffer in arrivals:
            arrived()
            waits.append(to_cell(buffer.at[part_in], buffer.at[part_out], 2 * mate))
        return waits

    def embedding_pieces(k):
        pieces = []
        for q in range(n_q):
            start = pl.multiple_of(t * q_rows + q * BLOCK, BLOCK)
            pieces.append((emb.at[k + 1, pl.ds(start, BLOCK)], ys.at[k, :, pl.ds(q * BLOCK, BLOCK)]))
        return pieces

    y_arrivals = to_pair(embedding_pieces(1))

    local[6].wait()
    for wait in list_waits:
        wait()

    pair = lax.broadcasted_iota(jnp.int32, (n_src * n_tgt, 1), 0)
    src_id = c * n_src + pair // n_tgt
    slot = pair % n_tgt
    tgt_id = (c - 1 + slot // n_q) * n_src + t * n_q + slot % n_q
    for k in range(2):
        found = jnp.zeros((n_src * n_tgt, 1), F32)
        for step in range(tiles):
            hit = jnp.logical_and(
                lists[step, k, 0:1, :] == src_id, lists[step, k, 1:2, :] == tgt_id
            )
            found = found + jnp.sum(jnp.where(hit, 1.0, 0.0), axis=1, keepdims=True)
        bias[k] = jnp.broadcast_to(jnp.where(found > 0.0, 0.0, NEG), (n_src * n_tgt, BLOCK))

    def norm_row(block):
        wide = block.astype(F32)
        square = wide * wide
        folded = sum(square[:, e : e + BLOCK] for e in range(0, depth, BLOCK))
        return scale * jnp.sum(jnp.transpose(folded), axis=0, keepdims=True)

    def source_norms(k):
        @pl.loop(0, n_src)
        def _(b):
            x_norm[k, pl.ds(b, 1), :] = norm_row(xs[k, pl.ds(pl.multiple_of(b * BLOCK, BLOCK), BLOCK), :])

    def products(k, part):
        y = ys[k, part]
        for q in range(n_q):
            y_norm[k, part, q : q + 1, :] = norm_row(y[q * BLOCK : (q + 1) * BLOCK])

        @pl.loop(0, n_src // 2)
        def _(pair_index):
            x = xs[k, pl.ds(pl.multiple_of(pair_index * 2 * BLOCK, 2 * BLOCK), 2 * BLOCK), :]
            cross = lax.dot_general(x, y, NT, preferred_element_type=F32) * (2.0 * scale)
            crossed = lax.dot_general(y, x, NT, preferred_element_type=F32) * (2.0 * scale)
            for side in range(2):
                b = pair_index * 2 + side
                block = pl.ds(pl.multiple_of(b * BLOCK, BLOCK), BLOCK)
                own = slice(side * BLOCK, (side + 1) * BLOCK)
                for q in range(n_q):
                    j = part * n_q + q
                    shift = bias[k, pl.ds(b * n_tgt + j, 1), :]
                    other = slice(q * BLOCK, (q + 1) * BLOCK)
                    d[k, j, block, :] = cross[own, other] + shift
                    dt[k, b, pl.ds(pl.multiple_of(j * BLOCK, BLOCK), BLOCK), :] = crossed[other, own] + shift

    def fold(combine, slabs):
        value = functools.reduce(combine, slabs)
        while value.shape[0] > 1:
            middle = value.shape[0] // 2
            value = combine(value[:middle], value[middle:])
        return value

    def log_sum(terms, products_of, count):
        slabs = [
            (terms[b * BLOCK : (b + 1) * BLOCK, :] + products_of[b * BLOCK : (b + 1) * BLOCK, :]).reshape(
                BLOCK // 8, 8, BLOCK
            )
            for b in range(count)
        ]
        high = fold(jnp.maximum, slabs)
        mass = fold(jnp.add, [jnp.exp2(slab - high) for slab in slabs])[0]
        high = high[0]
        highest = jnp.max(high, axis=0, keepdims=True)
        return highest, jnp.sum(mass * jnp.exp2(high - highest), axis=0, keepdims=True)

    def down(target, values):
        count = values.shape[0]
        tall = jnp.transpose(jnp.concatenate([values] * (BLOCK // count), axis=0))
        for b in range(count):
            target[b * BLOCK : (b + 1) * BLOCK, :] = jnp.broadcast_to(tall[:, b : b + 1], (BLOCK, BLOCK))

    def row_pass(k, phase):
        filler = [jnp.zeros((8 - n_tgt, BLOCK), F32)]
        down(hb.at[k], jnp.concatenate([h_row[k, part, 0:n_q, :] for part in range(3)] + filler, axis=0))

        @pl.loop(0, n_src // 2)
        def _(pair_index):
            for side in range(2):
                b = pair_index * 2 + side
                highest, mass = log_sum(hb.at[k], dt.at[k, b], n_tgt)
                row_send[k, phase, 0, pl.ds(b, 1), :] = highest
                row_send[k, phase, 1, pl.ds(b, 1), :] = mass

        return [
            to_tile(row_send.at[k, phase], row_recv.at[k, phase, step - 1], step) for step in range(1, tiles)
        ]

    def merged(pairs):
        highest = functools.reduce(jnp.maximum, [pair[0] for pair in pairs])
        total = sum(pair[1] * jnp.exp2(pair[0] - highest) for pair in pairs)
        return highest + jnp.log(total) * LOG2E

    def row_total(k, phase, waits):
        for wait in waits:
            wait()
        pairs = [(row_send[k, phase, 0], row_send[k, phase, 1])]
        pairs += [(row_recv[k, phase, s, 0], row_recv[k, phase, s, 1]) for s in range(tiles - 1)]
        return merged(pairs)

    def spread(k, values):
        down(ub.at[k], values)

    def col_pass(k, phase, total):
        mass = jnp.concatenate(
            [log_mass[k : k + 1, b * BLOCK : (b + 1) * BLOCK] for b in range(n_src)], axis=0
        )
        spread(k, mass * LOG2E - LAM * total + (LAM - 1.0) * x_norm[k])

        @pl.loop(0, 3)
        def _(part):
            for q in range(n_q):
                highest, mass = log_sum(ub.at[k], d.at[k, part * n_q + q], n_src)
                col_send[k, phase, part, 0, q : q + 1, :] = highest
                col_send[k, phase, part, 1, q : q + 1, :] = mass

        mine = col_send.at[k, phase]
        return [
            to_cell(mine.at[pl.ds(1, 2)], col_near.at[k, phase, 0], 1),
            to_cell(mine.at[pl.ds(0, 2)], col_near.at[k, phase, 1], -1),
            to_cell(mine.at[pl.ds(2, 1)], col_far.at[k, phase, 0], 2),
            to_cell(mine.at[pl.ds(0, 1)], col_far.at[k, phase, 1], -2),
        ]

    def col_total(k, phase, waits):
        for wait in waits:
            wait()

        def pair(ref):
            return ref[0], ref[1]

        mine = col_send.at[k, phase]
        below, above = col_near.at[k, phase, 0], col_near.at[k, phase, 1]
        far_below, far_above = col_far.at[k, phase, 0, 0], col_far.at[k, phase, 1, 0]
        totals = (
            merged([pair(far_below), pair(below.at[0]), pair(mine.at[0])]),
            merged([pair(below.at[1]), pair(mine.at[1]), pair(above.at[0])]),
            merged([pair(mine.at[2]), pair(above.at[1]), pair(far_above)]),
        )
        for part in range(3):
            h_row[k, part] = lm_win[part, k] - LAM * totals[part] + (LAM - 1.0) * y_norm[k, part]

    y_norm[...] = jnp.zeros(y_norm.shape, F32)
    local[0].wait()
    local[1].wait()
    source_norms(1)
    products(1, 1)
    local[2].wait()
    local[3].wait()
    source_norms(0)
    products(0, 1)
    for wait in lm_waits:
        wait()
    row_waits, col_waits = {}, {}

    def first_rows(k, y_waits):
        products(k, part_in)
        for wait in y_waits:
            wait()
        products(k, part_out)
        for part in range(3):
            h_row[k, part] = lm_win[part, k] - y_norm[k, part]
        row_waits[k] = row_pass(k, 0)

    def columns(k, sweep):
        col_waits[k] = col_pass(k, sweep, row_total(k, sweep, row_waits[k]))

    def next_rows(k, sweep):
        col_total(k, sweep, col_waits[k])
        row_waits[k] = row_pass(k, sweep + 1)

    y_waits = hand_on(y_arrivals)
    y_arrivals = to_pair(embedding_pieces(0))
    first_rows(1, y_waits)
    y_waits = hand_on(y_arrivals)
    sig_arrivals = to_pair([(sig.at[t_rows], fates_1)])
    columns(1, 0)
    first_rows(0, y_waits)
    sig_waits = hand_on(sig_arrivals)
    for sweep in range(SWEEPS):
        next_rows(1, sweep)
        columns(0, sweep)
        if sweep + 1 < SWEEPS:
            columns(1, sweep + 1)
            next_rows(0, sweep)

    def weights(k, block, part):
        return jnp.concatenate(
            [
                jnp.exp2(
                    h_row[k, part, q : q + 1, :] + d[k, part * n_q + q, block, :] - ub[k, block, :]
                ).astype(BF16)
                for q in range(n_q)
            ],
            axis=1,
        )

    def row_block(index):
        return pl.ds(pl.multiple_of(index * q_rows, q_rows), q_rows)

    spread(1, row_total(1, SWEEPS, row_waits[1]))
    local[4].wait()
    for wait in sig_waits:
        wait()
    t_1 = t + 1 - 2 * lax.rem(t, 2)
    t_2 = lax.rem(t + 2, tiles)
    t_3 = lax.rem(t_1 + 2, tiles)
    half = fates_0.shape[3]
    lanes = [slice(f * half, (f + 1) * half) for f in range(2)]

    def late_part(index):
        block = row_block(index)
        return sum(
            jnp.dot(weights(1, block, part), fates_1[part], preferred_element_type=F32) for part in range(3)
        )

    def early_part(index, f):
        block = row_block(index)
        return sum(
            jnp.dot(w_0[part, block, :], fates_0[f, part], preferred_element_type=F32) for part in range(3)
        )

    def to_mate(k, f):
        return to_peer(a_send.at[k, f], a_recv.at[k, f], t_1)

    def across(k, f, arrived):
        arrived()
        b_send[k, f] = (kept[k, f, 1] + a_recv[k, f, 1].astype(F32)).astype(BF16)
        return to_peer(b_send.at[k, f], b_recv.at[k, f], t_2)

    def summed(k, f, arrived):
        arrived()
        return (kept[k, f, 0] + a_recv[k, f, 0].astype(F32) + b_recv[k, f].astype(F32)).astype(BF16)

    def gather(block, out, f):
        here = out.at[t_rows, lanes[f]]
        return to_peer(block, here, t_1), to_peer(block, here, t_2)

    def forward(waits, out, f):
        waits[1]()
        there = out.at[row_block(t_2), lanes[f]]
        return [waits[0], to_peer(there, there, t_1)]

    for i, index in enumerate((t_1, t_3)):
        total = late_part(index)
        for f in range(2):
            a_send[1, f, i] = total[:, lanes[f]].astype(BF16)
    a_waits = [to_mate(1, f) for f in range(2)]
    for i, index in enumerate((t, t_2)):
        total = late_part(index)
        for f in range(2):
            kept[1, f, i] = total[:, lanes[f]]
    b_waits = [across(1, f, a_waits[f]) for f in range(2)]

    next_rows(0, SWEEPS - 1)

    late_arrivals, late_gather = [], []
    for f in range(2):
        fates_0[f, 1] = summed(1, f, b_waits[f])
        late_arrivals.append(to_pair([(fates_0.at[f, 1], fates_0.at[f])]))
        late_gather.append(gather(fates_0.at[f, 1], late, f))
        late[t_rows, lanes[f]] = fates_0[f, 1]

    spread(0, row_total(0, SWEEPS, row_waits[0]))
    late_waits = [hand_on(late_arrivals[f]) for f in range(2)]

    @pl.loop(0, tiles)
    def _(r):
        block = row_block(r)
        for part in range(3):
            w_0[part, block, :] = weights(0, block, part)

    b_waits = []
    for f in range(2):
        for wait in late_waits[f]:
            wait()
        for i, index in enumerate((t_1, t_3)):
            a_send[0, f, i] = early_part(index, f).astype(BF16)
        arrived = to_mate(0, f)
        for i, index in enumerate((t, t_2)):
            kept[0, f, i] = early_part(index, f)
        b_waits.append(across(0, f, arrived))
    gather_waits = []
    for f in range(2):
        gather_waits += forward(late_gather[f], late, f)
    early_gather = []
    for f in range(2):
        early_own[f] = summed(0, f, b_waits[f])
        early_gather.append(gather(early_own.at[f], early, f))
        early[t_rows, lanes[f]] = early_own[f]
    for f in range(2):
        gather_waits += forward(early_gather[f], early, f)
    for wait in gather_waits:
        wait()
    for copy, offset in sends:
        if offset is None:
            copy.wait_send()
        else:

            @pl.when(present(offset))
            def _(copy=copy):
                copy.wait_send()


def on_device(tiles, embeddings, log_mass, signatures, tile_list):
    _, rows, depth = embeddings.shape
    fate = signatures.shape[1]
    q_rows = rows // tiles
    n_src = rows // BLOCK
    n_q = q_rows // BLOCK
    n_tgt = 3 * n_q
    vmem = pltpu.VMEM
    copies = copy_count(tiles)
    return pl.pallas_call(
        functools.partial(kernel, tiles),
        out_shape=(
            jax.ShapeDtypeStruct((rows, fate), BF16),
            jax.ShapeDtypeStruct((rows, fate), BF16),
        ),
        in_specs=[pl.BlockSpec(memory_space=pltpu.HBM)] * 4,
        out_specs=(pl.BlockSpec(memory_space=vmem), pl.BlockSpec(memory_space=vmem)),
        scratch_shapes=[
            vmem((2, rows, depth), BF16),
            vmem((2, 3, q_rows, depth), BF16),
            vmem((2, n_tgt, rows, BLOCK), F32),
            vmem((2, n_src, n_tgt * BLOCK, BLOCK), F32),
            vmem((3, q_rows, fate), BF16),
            vmem((2, 3, q_rows, fate // 2), BF16),
            vmem((3, rows, q_rows), BF16),
            vmem((tiles,) + tile_list.shape, jnp.int32),
            vmem(log_mass.shape, F32),
            vmem((2, 8, BLOCK), F32),
            vmem((3, 2, 8, BLOCK), F32),
            vmem((2, n_src * n_tgt, BLOCK), F32),
            vmem((2, n_src, BLOCK), F32),
            vmem((2, 3, 8, BLOCK), F32),
            vmem((2, 3, 8, BLOCK), F32),
            vmem((2, 8 * BLOCK, BLOCK), F32),
            vmem((2, rows, BLOCK), F32),
            vmem((2, SWEEPS + 1, 2, n_src, BLOCK), F32),
            vmem((2, SWEEPS + 1, tiles - 1, 2, n_src, BLOCK), F32),
            vmem((2, SWEEPS, 3, 2, 8, BLOCK), F32),
            vmem((2, SWEEPS, 2, 2, 2, 8, BLOCK), F32),
            vmem((2, SWEEPS, 2, 1, 2, 8, BLOCK), F32),
            vmem((2, 2, 2, q_rows, fate // 2), BF16),
            vmem((2, 2, 2, q_rows, fate // 2), BF16),
            vmem((2, 2, q_rows, fate // 2), BF16),
            vmem((2, 2, q_rows, fate // 2), BF16),
            vmem((2, 2, 2, q_rows, fate // 2), F32),
            vmem((2, q_rows, fate // 2), BF16),
            pltpu.SemaphoreType.DMA((copies,)),
            pltpu.SemaphoreType.DMA((copies,)),
            pltpu.SemaphoreType.DMA((7,)),
        ],
        compiler_params=pltpu.CompilerParams(
            collective_id=0, has_side_effects=True, vmem_limit_bytes=58 * 1024 * 1024
        ),
    )(embeddings, log_mass, signatures, tile_list)


def solution(mesh):
    in_specs = (
        P(None, "cells", None),
        P(None, "cells"),
        P("cells", None),
        P(None, None, ("cells", "tiles")),
    )
    out_specs = (P("cells", None), P("cells", None))
    return jax.shard_map(
        functools.partial(on_device, mesh.shape["tiles"]),
        mesh=mesh,
        in_specs=in_specs,
        out_specs=out_specs,
        check_vma=False,
    )
```

```python
import functools
import math

import jax
import jax.numpy as jnp
from jax import lax
from jax.experimental import pallas as pl
from jax.experimental.pallas import tpu as pltpu
from jax.sharding import PartitionSpec as P

BLOCK = 128
SWEEPS = 2
EPS = 0.01
RHO = 1.0
NEG = -1e30
LOG2E = math.log2(math.e)
LAM = RHO / (RHO + EPS)
F32 = jnp.float32
BF16 = jnp.bfloat16
NT = (((1,), (1,)), ((), ()))


def copy_count(tiles):
    return tiles * 12 + 48


def kernel(
    tiles,
    emb,
    log_mass_in,
    sig,
    listing,
    early,
    late,
    xs,
    ys,
    d,
    dt,
    fates_1,
    fates_0,
    w_0,
    lists,
    log_mass,
    lm_src,
    lm_win,
    bias,
    x_norm,
    y_norm,
    h_row,
    hb,
    ub,
    row_send,
    row_recv,
    col_send,
    col_near,
    col_far,
    a_send,
    a_recv,
    b_send,
    b_recv,
    kept,
    early_own,
    send_sem,
    recv_sem,
    local_sem,
):
    c = lax.axis_index("cells")
    t = lax.axis_index("tiles")
    n = lax.axis_size("cells")
    rows = xs.shape[1]
    depth = xs.shape[2]
    q_rows = ys.shape[2]
    n_src = rows // BLOCK
    n_q = q_rows // BLOCK
    n_tgt = 3 * n_q
    scale = LOG2E / (EPS * depth)
    t_rows = pl.ds(pl.multiple_of(t * q_rows, q_rows), q_rows)

    counter = [0]
    sends = []

    def fresh():
        counter[0] += 1
        return counter[0] - 1

    def present(offset):
        return jnp.logical_and(c + offset >= 0, c + offset < n)

    def to_tile(src, dst, step):
        return to_peer(src, dst, lax.rem(t + step, tiles))

    def to_peer(src, dst, peer):
        i = fresh()
        copy = pltpu.make_async_remote_copy(
            src_ref=src,
            dst_ref=dst,
            send_sem=send_sem.at[i],
            recv_sem=recv_sem.at[i],
            device_id={"tiles": peer},
            device_id_type=pl.DeviceIdType.MESH,
        )
        copy.start()
        sends.append((copy, None))
        return copy.wait_recv

    def to_cell(src, dst, offset, origin=None):
        origin = -offset if origin is None else origin
        i = fresh()
        copy = pltpu.make_async_remote_copy(
            src_ref=src,
            dst_ref=dst,
            send_sem=send_sem.at[i],
            recv_sem=recv_sem.at[i],
            device_id={"cells": c + offset},
            device_id_type=pl.DeviceIdType.MESH,
        )

        @pl.when(present(offset))
        def _():
            copy.start()

        sends.append((copy, offset))

        def wait():
            @pl.when(present(origin))
            def _():
                copy.wait_recv()

        return wait

    for offset, part in ((1, 0), (-1, 2)):

        @pl.when(jnp.logical_not(present(-offset)))
        def _(part=part):
            for k in range(2):
                ys[k, part] = jnp.zeros(ys.shape[2:], BF16)
            fates_1[part] = jnp.zeros(fates_1.shape[1:], BF16)
            for f in range(2):
                fates_0[f, part] = jnp.zeros(fates_0.shape[2:], BF16)
            lm_win[part] = jnp.zeros(lm_win.shape[1:], F32)

    for buffer in (col_near, col_far):
        buffer[:, :, :, :, 0] = jnp.full(buffer.shape[:4] + buffer.shape[5:], NEG, F32)
        buffer[:, :, :, :, 1] = jnp.zeros(buffer.shape[:4] + buffer.shape[5:], F32)
    col_send[:, :, :, 0] = jnp.full(col_send.shape[:3] + col_send.shape[4:], NEG, F32)
    col_send[:, :, :, 1] = jnp.ones(col_send.shape[:3] + col_send.shape[4:], F32)

    barrier = pltpu.get_barrier_semaphore()
    for step in range(1, tiles):
        pl.semaphore_signal(
            barrier, inc=1, device_id={"tiles": lax.rem(t + step, tiles)}, device_id_type=pl.DeviceIdType.MESH
        )
    for offset in (1, -1, 2, -2):

        @pl.when(present(offset))
        def _(offset=offset):
            pl.semaphore_signal(
                barrier, inc=1, device_id={"cells": c + offset}, device_id_type=pl.DeviceIdType.MESH
            )

    local = []
    for i, (src, dst) in enumerate(
        (
            (emb.at[1], xs.at[1]),
            (emb.at[2, t_rows], ys.at[1, 1]),
            (emb.at[0], xs.at[0]),
            (emb.at[1, t_rows], ys.at[0, 1]),
            (sig.at[t_rows], fates_1.at[1]),
            (log_mass_in, log_mass),
            (listing, lists.at[0]),
        )
    ):
        copy = pltpu.make_async_copy(src, dst, local_sem.at[i])
        copy.start()
        local.append(copy)

    local[5].wait()
    lm_src[...] = jnp.zeros(lm_src.shape, F32)
    for k in range(2):
        for q in range(n_q):
            lanes = pl.ds(pl.multiple_of((t * n_q + q) * BLOCK, BLOCK), BLOCK)
            lm_src[k, q : q + 1, :] = log_mass[k + 1 : k + 2, lanes] * LOG2E
    lm_win[1] = lm_src[...]

    peers = sum(present(offset).astype(jnp.int32) for offset in (1, -1, 2, -2))
    pl.semaphore_wait(barrier, tiles - 1 + peers)

    list_waits = [to_tile(listing, lists.at[step], step) for step in range(1, tiles)]
    near = ((1, 0), (-1, 2))
    lm_waits = [to_cell(lm_src, lm_win.at[part], offset) for offset, part in near]

    odd = lax.rem(c, 2)
    mate = 1 - 2 * odd
    part_in, part_out = 2 - 2 * odd, 2 * odd

    def to_pair(pieces):
        return [(to_cell(src, buffer.at[part_out], mate, mate), buffer) for src, buffer in pieces]

    def hand_on(arrivals):
        waits = []
        for arrived, buffer in arrivals:
            arrived()
            waits.append(to_cell(buffer.at[part_in], buffer.at[part_out], 2 * mate))
        return waits

    def embedding_pieces(k):
        pieces = []
        for q in range(n_q):
            start = pl.multiple_of(t * q_rows + q * BLOCK, BLOCK)
            pieces.append((emb.at[k + 1, pl.ds(start, BLOCK)], ys.at[k, :, pl.ds(q * BLOCK, BLOCK)]))
        return pieces

    y_waits = [to_cell(emb.at[2, t_rows], ys.at[1, part], offset) for offset, part in near]

    local[6].wait()
    for wait in list_waits:
        wait()

    pair = lax.broadcasted_iota(jnp.int32, (n_src * n_tgt, 1), 0)
    src_id = c * n_src + pair // n_tgt
    slot = pair % n_tgt
    tgt_id = (c - 1 + slot // n_q) * n_src + t * n_q + slot % n_q
    for k in range(2):
        found = jnp.zeros((n_src * n_tgt, 1), F32)
        for step in range(tiles):
            hit = jnp.logical_and(
                lists[step, k, 0:1, :] == src_id, lists[step, k, 1:2, :] == tgt_id
            )
            found = found + jnp.sum(jnp.where(hit, 1.0, 0.0), axis=1, keepdims=True)
        bias[k] = jnp.broadcast_to(jnp.where(found > 0.0, 0.0, NEG), (n_src * n_tgt, BLOCK))

    def norm_row(block):
        wide = block.astype(F32)
        square = wide * wide
        folded = sum(square[:, e : e + BLOCK] for e in range(0, depth, BLOCK))
        return scale * jnp.sum(jnp.transpose(folded), axis=0, keepdims=True)

    def source_norms(k):
        @pl.loop(0, n_src)
        def _(b):
            x_norm[k, pl.ds(b, 1), :] = norm_row(xs[k, pl.ds(pl.multiple_of(b * BLOCK, BLOCK), BLOCK), :])

    def products(k, part):
        y = ys[k, part]
        for q in range(n_q):
            y_norm[k, part, q : q + 1, :] = norm_row(y[q * BLOCK : (q + 1) * BLOCK])

        @pl.loop(0, n_src // 2)
        def _(pair_index):
            x = xs[k, pl.ds(pl.multiple_of(pair_index * 2 * BLOCK, 2 * BLOCK), 2 * BLOCK), :]
            cross = lax.dot_general(x, y, NT, preferred_element_type=F32) * (2.0 * scale)
            crossed = lax.dot_general(y, x, NT, preferred_element_type=F32) * (2.0 * scale)
            for side in range(2):
                b = pair_index * 2 + side
                block = pl.ds(pl.multiple_of(b * BLOCK, BLOCK), BLOCK)
                own = slice(side * BLOCK, (side + 1) * BLOCK)
                for q in range(n_q):
                    j = part * n_q + q
                    shift = bias[k, pl.ds(b * n_tgt + j, 1), :]
                    other = slice(q * BLOCK, (q + 1) * BLOCK)
                    d[k, j, block, :] = cross[own, other] + shift
                    dt[k, b, pl.ds(pl.multiple_of(j * BLOCK, BLOCK), BLOCK), :] = crossed[other, own] + shift

    def fold(combine, slabs):
        value = functools.reduce(combine, slabs)
        while value.shape[0] > 1:
            middle = value.shape[0] // 2
            value = combine(value[:middle], value[middle:])
        return value

    def log_sum(terms, products_of, count):
        slabs = [
            (terms[b * BLOCK : (b + 1) * BLOCK, :] + products_of[b * BLOCK : (b + 1) * BLOCK, :]).reshape(
                BLOCK // 8, 8, BLOCK
            )
            for b in range(count)
        ]
        high = fold(jnp.maximum, slabs)
        mass = fold(jnp.add, [jnp.exp2(slab - high) for slab in slabs])[0]
        high = high[0]
        highest = jnp.max(high, axis=0, keepdims=True)
        return highest, jnp.sum(mass * jnp.exp2(high - highest), axis=0, keepdims=True)

    def down(row):
        return jnp.transpose(jnp.broadcast_to(row, (BLOCK, BLOCK)))

    def row_pass(k, phase):
        for j in range(n_tgt):
            hb[k, j * BLOCK : (j + 1) * BLOCK, :] = down(h_row[k, j // n_q, j % n_q : j % n_q + 1, :])

        @pl.loop(0, n_src // 2)
        def _(pair_index):
            for side in range(2):
                b = pair_index * 2 + side
                highest, mass = log_sum(hb.at[k], dt.at[k, b], n_tgt)
                row_send[k, phase, 0, pl.ds(b, 1), :] = highest
                row_send[k, phase, 1, pl.ds(b, 1), :] = mass

        return [
            to_tile(row_send.at[k, phase], row_recv.at[k, phase, step - 1], step) for step in range(1, tiles)
        ]

    def merged(pairs):
        highest = functools.reduce(jnp.maximum, [pair[0] for pair in pairs])
        total = sum(pair[1] * jnp.exp2(pair[0] - highest) for pair in pairs)
        return highest + jnp.log(total) * LOG2E

    def row_total(k, phase, waits):
        for wait in waits:
            wait()
        pairs = [(row_send[k, phase, 0], row_send[k, phase, 1])]
        pairs += [(row_recv[k, phase, s, 0], row_recv[k, phase, s, 1]) for s in range(tiles - 1)]
        return merged(pairs)

    def spread(k, values):
        for b in range(n_src):
            ub[k, b * BLOCK : (b + 1) * BLOCK, :] = down(values[b : b + 1])

    def col_pass(k, phase, total):
        mass = jnp.concatenate(
            [log_mass[k : k + 1, b * BLOCK : (b + 1) * BLOCK] for b in range(n_src)], axis=0
        )
        spread(k, mass * LOG2E - LAM * total + (LAM - 1.0) * x_norm[k])

        @pl.loop(0, 3)
        def _(part):
            for q in range(n_q):
                highest, mass = log_sum(ub.at[k], d.at[k, part * n_q + q], n_src)
                col_send[k, phase, part, 0, q : q + 1, :] = highest
                col_send[k, phase, part, 1, q : q + 1, :] = mass

        mine = col_send.at[k, phase]
        return [
            to_cell(mine.at[pl.ds(1, 2)], col_near.at[k, phase, 0], 1),
            to_cell(mine.at[pl.ds(0, 2)], col_near.at[k, phase, 1], -1),
            to_cell(mine.at[pl.ds(2, 1)], col_far.at[k, phase, 0], 2),
            to_cell(mine.at[pl.ds(0, 1)], col_far.at[k, phase, 1], -2),
        ]

    def col_total(k, phase, waits):
        for wait in waits:
            wait()

        def pair(ref):
            return ref[0], ref[1]

        mine = col_send.at[k, phase]
        below, above = col_near.at[k, phase, 0], col_near.at[k, phase, 1]
        far_below, far_above = col_far.at[k, phase, 0, 0], col_far.at[k, phase, 1, 0]
        totals = (
            merged([pair(far_below), pair(below.at[0]), pair(mine.at[0])]),
            merged([pair(below.at[1]), pair(mine.at[1]), pair(above.at[0])]),
            merged([pair(mine.at[2]), pair(above.at[1]), pair(far_above)]),
        )
        for part in range(3):
            h_row[k, part] = lm_win[part, k] - LAM * totals[part] + (LAM - 1.0) * y_norm[k, part]

    y_norm[...] = jnp.zeros(y_norm.shape, F32)
    local[0].wait()
    local[1].wait()
    source_norms(1)
    products(1, 1)
    local[2].wait()
    local[3].wait()
    source_norms(0)
    products(0, 1)
    for wait in lm_waits:
        wait()
    row_waits, col_waits = {}, {}

    def first_rows(k):
        for part in (part_in, part_out):
            products(k, part)
        for part in range(3):
            h_row[k, part] = lm_win[part, k] - y_norm[k, part]
        row_waits[k] = row_pass(k, 0)

    def columns(k, sweep):
        col_waits[k] = col_pass(k, sweep, row_total(k, sweep, row_waits[k]))

    def next_rows(k, sweep):
        col_total(k, sweep, col_waits[k])
        row_waits[k] = row_pass(k, sweep + 1)

    for wait in y_waits:
        wait()
    y_arrivals = to_pair(embedding_pieces(0))
    first_rows(1)
    y_waits = hand_on(y_arrivals)
    sig_arrivals = to_pair([(sig.at[t_rows], fates_1)])
    columns(1, 0)
    for wait in y_waits:
        wait()
    first_rows(0)
    sig_waits = hand_on(sig_arrivals)
    for sweep in range(SWEEPS):
        next_rows(1, sweep)
        columns(0, sweep)
        if sweep + 1 < SWEEPS:
            columns(1, sweep + 1)
            next_rows(0, sweep)

    def weights(k, block, part):
        return jnp.concatenate(
            [
                jnp.exp2(
                    h_row[k, part, q : q + 1, :] + d[k, part * n_q + q, block, :] - ub[k, block, :]
                ).astype(BF16)
                for q in range(n_q)
            ],
            axis=1,
        )

    def row_block(index):
        return pl.ds(pl.multiple_of(index * q_rows, q_rows), q_rows)

    spread(1, row_total(1, SWEEPS, row_waits[1]))
    local[4].wait()
    for wait in sig_waits:
        wait()
    t_1 = t + 1 - 2 * lax.rem(t, 2)
    t_2 = lax.rem(t + 2, tiles)
    t_3 = lax.rem(t_1 + 2, tiles)
    half = fates_0.shape[3]
    lanes = [slice(f * half, (f + 1) * half) for f in range(2)]

    def late_part(index):
        block = row_block(index)
        return sum(
            jnp.dot(weights(1, block, part), fates_1[part], preferred_element_type=F32) for part in range(3)
        )

    def early_part(index, f):
        block = row_block(index)
        return sum(
            jnp.dot(w_0[part, block, :], fates_0[f, part], preferred_element_type=F32) for part in range(3)
        )

    def to_mate(k, f):
        return to_peer(a_send.at[k, f], a_recv.at[k, f], t_1)

    def across(k, f, arrived):
        arrived()
        b_send[k, f] = (kept[k, f, 1] + a_recv[k, f, 1].astype(F32)).astype(BF16)
        return to_peer(b_send.at[k, f], b_recv.at[k, f], t_2)

    def summed(k, f, arrived):
        arrived()
        return (kept[k, f, 0] + a_recv[k, f, 0].astype(F32) + b_recv[k, f].astype(F32)).astype(BF16)

    def gather(block, out, f):
        here = out.at[t_rows, lanes[f]]
        return to_peer(block, here, t_1), to_peer(block, here, t_2)

    def forward(waits, out, f):
        waits[1]()
        there = out.at[row_block(t_2), lanes[f]]
        return [waits[0], to_peer(there, there, t_1)]

    for i, index in enumerate((t_1, t_3)):
        total = late_part(index)
        for f in range(2):
            a_send[1, f, i] = total[:, lanes[f]].astype(BF16)
    a_waits = [to_mate(1, f) for f in range(2)]
    for i, index in enumerate((t, t_2)):
        total = late_part(index)
        for f in range(2):
            kept[1, f, i] = total[:, lanes[f]]
    b_waits = [across(1, f, a_waits[f]) for f in range(2)]

    next_rows(0, SWEEPS - 1)

    late_waits, late_gather = [], []
    for f in range(2):
        fates_0[f, 1] = summed(1, f, b_waits[f])
        late_waits.append([to_cell(fates_0.at[f, 1], fates_0.at[f, part], offset) for offset, part in near])
        late_gather.append(gather(fates_0.at[f, 1], late, f))
        late[t_rows, lanes[f]] = fates_0[f, 1]

    spread(0, row_total(0, SWEEPS, row_waits[0]))

    @pl.loop(0, tiles)
    def _(r):
        block = row_block(r)
        for part in range(3):
            w_0[part, block, :] = weights(0, block, part)

    b_waits = []
    for f in range(2):
        for wait in late_waits[f]:
            wait()
        for i, index in enumerate((t_1, t_3)):
            a_send[0, f, i] = early_part(index, f).astype(BF16)
        arrived = to_mate(0, f)
        for i, index in enumerate((t, t_2)):
            kept[0, f, i] = early_part(index, f)
        b_waits.append(across(0, f, arrived))
    gather_waits = []
    for f in range(2):
        gather_waits += forward(late_gather[f], late, f)
    early_gather = []
    for f in range(2):
        early_own[f] = summed(0, f, b_waits[f])
        early_gather.append(gather(early_own.at[f], early, f))
        early[t_rows, lanes[f]] = early_own[f]
    for f in range(2):
        gather_waits += forward(early_gather[f], early, f)
    for wait in gather_waits:
        wait()
    for copy, offset in sends:
        if offset is None:
            copy.wait_send()
        else:

            @pl.when(present(offset))
            def _(copy=copy):
                copy.wait_send()


def on_device(tiles, embeddings, log_mass, signatures, tile_list):
    _, rows, depth = embeddings.shape
    fate = signatures.shape[1]
    q_rows = rows // tiles
    n_src = rows // BLOCK
    n_q = q_rows // BLOCK
    n_tgt = 3 * n_q
    vmem = pltpu.VMEM
    copies = copy_count(tiles)
    return pl.pallas_call(
        functools.partial(kernel, tiles),
        out_shape=(
            jax.ShapeDtypeStruct((rows, fate), BF16),
            jax.ShapeDtypeStruct((rows, fate), BF16),
        ),
        in_specs=[pl.BlockSpec(memory_space=pltpu.HBM)] * 4,
        out_specs=(pl.BlockSpec(memory_space=vmem), pl.BlockSpec(memory_space=vmem)),
        scratch_shapes=[
            vmem((2, rows, depth), BF16),
            vmem((2, 3, q_rows, depth), BF16),
            vmem((2, n_tgt, rows, BLOCK), F32),
            vmem((2, n_src, n_tgt * BLOCK, BLOCK), F32),
            vmem((3, q_rows, fate), BF16),
            vmem((2, 3, q_rows, fate // 2), BF16),
            vmem((3, rows, q_rows), BF16),
            vmem((tiles,) + tile_list.shape, jnp.int32),
            vmem(log_mass.shape, F32),
            vmem((2, 8, BLOCK), F32),
            vmem((3, 2, 8, BLOCK), F32),
            vmem((2, n_src * n_tgt, BLOCK), F32),
            vmem((2, n_src, BLOCK), F32),
            vmem((2, 3, 8, BLOCK), F32),
            vmem((2, 3, 8, BLOCK), F32),
            vmem((2, n_tgt * BLOCK, BLOCK), F32),
            vmem((2, rows, BLOCK), F32),
            vmem((2, SWEEPS + 1, 2, n_src, BLOCK), F32),
            vmem((2, SWEEPS + 1, tiles - 1, 2, n_src, BLOCK), F32),
            vmem((2, SWEEPS, 3, 2, 8, BLOCK), F32),
            vmem((2, SWEEPS, 2, 2, 2, 8, BLOCK), F32),
            vmem((2, SWEEPS, 2, 1, 2, 8, BLOCK), F32),
            vmem((2, 2, 2, q_rows, fate // 2), BF16),
            vmem((2, 2, 2, q_rows, fate // 2), BF16),
            vmem((2, 2, q_rows, fate // 2), BF16),
            vmem((2, 2, q_rows, fate // 2), BF16),
            vmem((2, 2, 2, q_rows, fate // 2), F32),
            vmem((2, q_rows, fate // 2), BF16),
            pltpu.SemaphoreType.DMA((copies,)),
            pltpu.SemaphoreType.DMA((copies,)),
            pltpu.SemaphoreType.DMA((7,)),
        ],
        compiler_params=pltpu.CompilerParams(
            collective_id=0, has_side_effects=True, vmem_limit_bytes=58 * 1024 * 1024
        ),
    )(embeddings, log_mass, signatures, tile_list)


def solution(mesh):
    in_specs = (
        P(None, "cells", None),
        P(None, "cells"),
        P("cells", None),
        P(None, None, ("cells", "tiles")),
    )
    out_specs = (P("cells", None), P("cells", None))
    return jax.shard_map(
        functools.partial(on_device, mesh.shape["tiles"]),
        mesh=mesh,
        in_specs=in_specs,
        out_specs=out_specs,
        check_vma=False,
    )
```
